256 devices in a mesh: grp: 16 (over y, x_hi, core), tp: 16 (over x_lo, z).
Axes of the slice: x: 4 (x_hi: 2, x_lo: 2; x = x_hi * 2 + x_lo), y: 4, z: 8, core: 2. Of those that a mesh axis runs over, the one named last changes fastest.
Arguments:
- tokens: bfloat16 [8192, 16384], P('grp', 'tp'), may hold values from -6 to 6
- kv_weight: bfloat16 [16384, 2048], P('tp'), may hold values from -0.046875 to 0.046875
- down_projection_factors: bfloat16 [16384, 2048], P('tp', 'grp'), may hold values from -0.046875 to 0.046875
- up_projection_factors: bfloat16 [2048, 2048], P('grp', 'tp'), may hold values from -0.125 to 0.125
- cotangent: bfloat16 [8192, 2048], P('grp', 'tp'), may hold values from -6 to 6
- adapter_ids: int32 [8192], P('grp'), may hold values from 0 to 31, as said below
- owner_slot: int32 [32], replicated, may hold values from 0 to 31, each once
Outputs:
- key_value_output: bfloat16 [8192, 2048], P('grp', 'tp')
- token_input_gradient: bfloat16 [8192, 16384], P('grp', 'tp')
- down_grad: float32 [16384, 2048], P('tp', 'grp')
- up_factor_gradient: float32 [2048, 2048], P('grp', 'tp')
The draws below stay inside these ranges and needn't reach their ends.
Inputs may be any that keep to these rules, and one draw needn't show every extreme that they name: `adapter_ids`: tokens come in aligned sequences of 64 that share one adapter; every adapter has at least one sequence. `owner_slot`: every slot holds exactly one adapter.
All inputs are finite; a program needn't handle non-finite values.
Results may differ from the reference program's by a relative error of at most 0.0031.
Values may be sent and summed in bfloat16 or wider, within the bound.
A program may use at most 128 MiB of HBM per device.

```python
import jax
import jax.numpy as jnp
from jax import lax

D = 16384
RANK = 64
RUN = 64
ADAPTERS = 32
TOKENS = 8192
KV_COLS = 2048


def draw_adapter_ids(key, part):
    key = jax.random.fold_in(key, 7)
    first_key, rest_key, order_key = jax.random.split(key, 3)
    run_count = TOKENS // RUN
    covered = jax.random.permutation(first_key, ADAPTERS).astype(jnp.int32)
    others = jax.random.randint(rest_key, (run_count - ADAPTERS,), 0, ADAPTERS, dtype=jnp.int32)
    run_ids = jnp.concatenate([covered, others])
    run_ids = jax.random.permutation(order_key, run_ids)
    return jnp.repeat(run_ids, RUN, total_repeat_length=TOKENS).astype(jnp.int32)


def steps_of(stream_key, shape, cuts, smallest, high):
    factor_of, own = 1.0, jax.random.fold_in(stream_key, 6)
    for axis_at, shards_of in cuts:
        heights = jnp.exp(jax.random.uniform(jax.random.fold_in(own, axis_at), (shards_of,), jnp.float32, smallest / len(cuts), high / len(cuts)))
        factor_of = factor_of * jnp.repeat(heights, shape[axis_at] // shards_of).reshape([-1 if axis == axis_at else 1 for axis in range(len(shape))])
    return factor_of


def centred(rng, shape, spread, most, pieces=(), held_as=jnp.bfloat16):
    array = spread * jax.random.normal(rng, shape, jnp.float32)
    if pieces:
        array = array * steps_of(rng, shape, pieces, -0.22, 0.18)
    return jnp.clip(array, -most, most).astype(held_as)


def setup_inputs(seed: int = 0) -> dict:
    splits = jax.random.split(jax.random.key(seed), 8)
    tokens = centred(splits[0], (TOKENS, D), 1.0, 6.0, ((0, 16), (1, 16)))
    kv_weight = centred(splits[1], (D, KV_COLS), D ** -0.5, 0.046875, ((0, 16),))
    down_projection_factors = centred(splits[2], (D, ADAPTERS * RANK), D ** -0.5, 0.046875, ((0, 16), (1, 16)))
    up_projection_factors = centred(splits[3], (ADAPTERS * RANK, KV_COLS), KV_COLS ** -0.5, 0.125, ((0, 16), (1, 16)))
    cotangent = centred(splits[4], (TOKENS, KV_COLS), 1.0, 6.0, ((0, 16), (1, 16)))
    adapter_ids = draw_adapter_ids(jax.random.fold_in(splits[7], 71), 0)
    owner_slot = jax.random.permutation(splits[6], ADAPTERS).astype(jnp.int32)
    return {"tokens": tokens, "kv_weight": kv_weight, "down_projection_factors": down_projection_factors, "up_projection_factors": up_projection_factors, "cotangent": cotangent, "adapter_ids": adapter_ids, "owner_slot": owner_slot}


adapter_scaling = 0.5


def reference(tokens, kv_weight, down_projection_factors, up_projection_factors, cotangent, adapter_ids, owner_slot):
    slots = owner_slot[adapter_ids].astype(jnp.int32)
    slot_selector = (slots[:, None] == jnp.arange(ADAPTERS, dtype=jnp.int32)[None, :]).astype(jnp.float32)
    select_half = slot_selector.astype(jnp.bfloat16)
    frozen_projection = jnp.dot(tokens, kv_weight, preferred_element_type=jnp.float32)
    lowered = jnp.dot(tokens, down_projection_factors, preferred_element_type=jnp.float32).reshape(TOKENS, ADAPTERS, RANK)
    down_rows = jnp.einsum("ux,uxn->un", slot_selector, lowered).astype(jnp.bfloat16)
    down_dispersed = (select_half[:, :, None] * down_rows[:, None, :]).reshape(TOKENS, ADAPTERS * RANK)
    key_value_output = (frozen_projection + adapter_scaling * jnp.dot(down_dispersed, up_projection_factors, preferred_element_type=jnp.float32)).astype(jnp.bfloat16)
    lifted_result = lax.dot_general(cotangent, up_projection_factors, (((1,), (1,)), ((), ())), preferred_element_type=jnp.float32)
    lifted_result = lifted_result.reshape(TOKENS, ADAPTERS, RANK)
    backward_row_block = (adapter_scaling * jnp.einsum("ux,uxn->un", slot_selector, lifted_result)).astype(jnp.bfloat16)
    backward_dispersed = (select_half[:, :, None] * backward_row_block[:, None, :]).reshape(TOKENS, ADAPTERS * RANK)
    token_frozen_output = lax.dot_general(cotangent, kv_weight, (((1,), (1,)), ((), ())), preferred_element_type=jnp.float32)
    token_adapter_output = lax.dot_general(backward_dispersed, down_projection_factors, (((1,), (1,)), ((), ())), preferred_element_type=jnp.float32)
    token_input_gradient = (token_frozen_output + token_adapter_output).astype(jnp.bfloat16)
    down_grad = lax.dot_general(tokens, backward_dispersed, (((0,), (0,)), ((), ())), preferred_element_type=jnp.float32)
    up_factor_gradient = adapter_scaling * lax.dot_general(down_dispersed, cotangent, (((0,), (0,)), ((), ())), preferred_element_type=jnp.float32)
    return key_value_output, token_input_gradient, down_grad, up_factor_gradient
```

```python
import jax
import jax.numpy as jnp
from jax import lax
from jax.experimental import pallas as pl
from jax.experimental.pallas import tpu as pltpu
from jax.sharding import PartitionSpec as P

MESH = pl.DeviceIdType.MESH
F32 = jnp.float32
BF16 = jnp.bfloat16
ROWS = 512
WIDTH = 1024
COLS = 2048
LANES = 128
RUN = 64
RUNS = 8
ZN = 8
YN = 4
EXTRA = 16
LEVELS = 32000.0
HALF_ROWS = ROWS // 2
Y_ORDER = ((2, 0), (2, 1), (1, 0), (1, 1), (3, 0), (3, 1), (0, 0), (0, 1))


def nt(a, b):
    return lax.dot_general(a, b, (((1,), (1,)), ((), ())), preferred_element_type=F32)


def nn(a, b):
    return jnp.dot(a, b, preferred_element_type=F32)


def encode(x, ref):
    rows = x.shape[0]
    top = jnp.maximum(jnp.max(jnp.abs(x), axis=0, keepdims=True), 1e-30)
    exponent = jnp.ceil(jnp.log2(top) + 1e-4)
    scaled = x * (jnp.exp2(-exponent) * LEVELS)
    ref[0:rows, :] = jnp.round(scaled).astype(jnp.int32).astype(jnp.int16)
    ref[rows : rows + EXTRA, :] = jnp.broadcast_to(
        exponent.astype(jnp.int32), (EXTRA, LANES)
    ).astype(jnp.int16)


def decode(ref, rows):
    exponent = ref[rows : rows + EXTRA, :].astype(jnp.int32).astype(F32)[0:1]
    scale = jnp.exp2(exponent) * (1.0 / LEVELS)
    return ref[0:rows, :].astype(jnp.int32).astype(F32) * scale


def kernel(
    ids,
    owner,
    tok_h,
    kv_h,
    df_h,
    uf_h,
    cot_h,
    kvo_h,
    tg_h,
    dg_h,
    ug_h,
    tok,
    kv,
    cot,
    cotf,
    dfull,
    ufull,
    tok_t,
    cot_t,
    acc,
    xs,
    xr,
    zs_half,
    zr_half,
    zs,
    zr,
    part_b,
    recv_b,
    tot_b,
    part_d,
    recv_d,
    tot_d,
    half_b,
    half_d,
    gacc,
    gcs,
    gcr,
    gys,
    gyr,
    gxs,
    gxr,
    uacc,
    ucs,
    ucr,
    udr,
    kvo,
    tg,
    dg,
    ug,
    load_sem,
    out_sem,
    u_s,
    u_r,
    d_s,
    d_r,
    c_s,
    c_r,
    x_s,
    x_r,
    z_s,
    z_r,
    p_s,
    p_r,
    gc_s,
    gc_r,
    gy_s,
    gy_r,
    gx_s,
    gx_r,
    uc_s,
    uc_r,
    ud_s,
    ud_r,
):
    g = lax.axis_index("grp")
    t = lax.axis_index("tp")
    y, xh, c = g // 4, (g // 2) % 2, g % 2
    xl, z = t // ZN, t % ZN

    def gi(dy, dx, dc):
        return ((y + dy) % YN) * 4 + ((xh + dx) % 2) * 2 + (c + dc) % 2

    def ti(dx, dz):
        return ((xl + dx) % 2) * ZN + (z + dz) % ZN

    def send(src, dst, ssem, rsem, to):
        pltpu.make_async_remote_copy(
            src_ref=src, dst_ref=dst, send_sem=ssem, recv_sem=rsem, device_id=to, device_id_type=MESH
        ).start()

    def wait(ref, sem):
        pltpu.make_async_copy(ref, ref, sem).wait()

    def cols(i):
        return pl.ds(pl.multiple_of(i * LANES, LANES), LANES)

    loads = [
        pltpu.make_async_copy(uf_h, ufull.at[g], load_sem.at[0]),
        pltpu.make_async_copy(cot_h, cot, load_sem.at[1]),
        pltpu.make_async_copy(tok_h, tok, load_sem.at[2]),
        pltpu.make_async_copy(kv_h, kv, load_sem.at[3]),
        pltpu.make_async_copy(df_h, dfull.at[g], load_sem.at[4]),
        pltpu.make_async_copy(cot_h, cotf.at[:, cols(t)], load_sem.at[5]),
    ]
    for copy in loads:
        copy.start()

    barrier = pltpu.get_barrier_semaphore()
    for k in range(1, 16):
        pl.semaphore_signal(barrier, inc=1, device_id=(g, (t + k) % 16), device_id_type=MESH)
    for dy, dx in Y_ORDER[:-2] + ((0, 1),):
        pl.semaphore_signal(barrier, inc=1, device_id=(gi(dy, dx, 0), t), device_id_type=MESH)
    pl.semaphore_signal(barrier, inc=1, device_id=(gi(0, 0, 1), t), device_id_type=MESH)
    pl.semaphore_wait(barrier, 15 + 7 + 1)

    x_peer_g = (gi(0, 1, 0), t)
    core_peer = (gi(0, 0, 1), t)
    y_up, y_down = (gi(1, 0, 0), t), (gi(3, 0, 0), t)
    x_peer_t = (g, ti(1, 0))
    z_up, z_down = (g, ti(0, 1)), (g, ti(0, 7))

    class Gather:
        def __init__(self, own, full, ssem, rsem):
            self.own, self.full, self.ssem, self.rsem, self.sent = own, full, ssem, rsem, 0

        def slot(self, index):
            return gi((index // 2) % 4, index % 2, index // 8)

        def push(self, slot, to, index, src=None):
            src = self.full.at[slot] if src is None else src
            send(src, self.full.at[slot], self.ssem.at[self.sent], self.rsem.at[index], to)
            self.sent += 1

        def begin(self):
            self.push(g, x_peer_g, 1, self.own)
            self.push(g, y_up, 6, self.own)
            self.push(g, y_down, 2, self.own)
            self.push(g, core_peer, 8, self.own)

        def got(self, index):
            wait(self.full.at[self.slot(index)], self.rsem.at[index])

        def handle(self, index):
            self.got(index)
            slot = self.slot(index)
            if index == 1:
                self.push(slot, y_up, 7)
                self.push(slot, y_down, 3)
            if index == 6:
                self.push(slot, y_up, 4)
            if index == 3:
                self.push(slot, y_down, 5)
            self.push(slot, core_peer, 8 + index)

        def drain(self):
            for i in range(self.sent):
                wait(self.own, self.ssem.at[i])

    up = Gather(uf_h, ufull, u_s, u_r)
    down = Gather(df_h, dfull, d_s, d_r)
    up.begin()

    sent_c = [0]

    def push_c(origin, to, index, src=None):
        dst = cotf.at[:, cols(origin)]
        send(dst if src is None else src, dst, c_s.at[sent_c[0]], c_r.at[index], to)
        sent_c[0] += 1

    def handle_c(index):
        dx, dz = index // 8, index % 8
        origin = ti(dx, dz)
        wait(cotf.at[:, cols(origin)], c_r.at[index])
        if index == 8:
            push_c(origin, z_up, 15)
            push_c(origin, z_down, 9)
        elif dz in (7, 6) or (dz == 5 and dx == 0):
            push_c(origin, z_up, index - 1)
        elif dz in (1, 2) or (dz == 3 and dx == 1):
            push_c(origin, z_down, index + 1)

    push_c(t, x_peer_t, 8, cot_h)
    push_c(t, z_up, 7, cot_h)
    push_c(t, z_down, 1, cot_h)
    down.begin()

    loads[2].wait()
    loads[3].wait()

    def dz_of(k):
        return (k % 2) * (3 - k // 2) + (1 - k % 2) * (4 + k // 2)

    def base_out(k, carry):
        x = nn(tok[...], kv[:, cols(ti(1, dz_of(k)))])
        encode(x, xs.at[k])
        send(xs.at[k], xr.at[k], x_s.at[k], x_r.at[k], x_peer_t)
        return carry

    lax.fori_loop(0, 8, base_out, 0)

    up.handle(1)

    def base_own(k, carry):
        acc[k] = nn(tok[...], kv[:, cols(ti(0, dz_of(k)))])
        return carry

    lax.fori_loop(0, 8, base_own, 0)

    for index in (6, 2, 7, 3):
        up.handle(index)

    lanes = lax.broadcasted_iota(jnp.int32, (RUN, LANES), 1)
    upper = lanes // RUN
    slots = [owner[ids[r * RUN]] for r in range(RUNS)]
    pairs = [s // 2 for s in slots]
    sides = [s % 2 for s in slots]

    handle_c(8)
    handle_c(7)
    handle_c(1)
    down.handle(6)
    down.handle(2)
    for index in (4, 5):
        up.handle(index)
    loads[0].wait()
    loads[1].wait()
    for index in range(8, 16):
        up.got(index)

    def pack(products, part):
        for q in range(RUNS // 2):
            both = []
            for r in (q, q + RUNS // 2):
                x = jnp.where(upper == sides[r], products(r), 0.0)
                both.append(x + pltpu.roll(x, RUN, 1))
            part[q * RUN : (q + 1) * RUN, :] = jnp.where(upper == 0, both[0], both[1])

    def reduce_start(part, recv, n):
        def body(k, carry):
            peer = (t + k) % 16
            rows = pl.ds(pl.multiple_of(peer * 16, 16), 16)
            send(part.at[rows, :], recv.at[t], p_s.at[2 * n], p_r.at[2 * n], (g, peer))
            return carry

        lax.fori_loop(1, 16, body, 0)
        recv[t] = part[pl.ds(pl.multiple_of(t * 16, 16), 16), :]

    def reduce_mid(recv, tot, n, scale):
        wait(recv.at[0:15], p_r.at[2 * n])
        rows = pl.ds(pl.multiple_of(t * 16, 16), 16)
        tot[rows, :] = (scale * jnp.sum(recv[...], axis=0)).astype(BF16)

        def body(k, carry):
            send(tot.at[rows, :], tot.at[rows, :], p_s.at[2 * n + 1], p_r.at[2 * n + 1], (g, (t + k) % 16))
            return carry

        lax.fori_loop(1, 16, body, 0)

    def reduce_end(tot, half, n):
        wait(tot.at[0:240, :], p_r.at[2 * n + 1])
        for q in range(RUNS // 2):
            both = tot[q * RUN : (q + 1) * RUN, :].astype(F32)
            for side, r in ((0, q), (1, q + RUNS // 2)):
                x = jnp.where(upper == side, both, 0.0)
                x = x + pltpu.roll(x, RUN, 1)
                half[r * RUN : (r + 1) * RUN, :] = jnp.where(upper == sides[r], x, 0.0).astype(BF16)

    def run_rows(r):
        return slice(r * RUN, (r + 1) * RUN)

    pack(lambda r: nt(cot[run_rows(r), :], ufull[pairs[r]]), part_b)
    reduce_start(part_b, recv_b, 0)

    tok_t[...] = tok[...].T
    cot_t[...] = cot[...].T

    handle_c(15)
    handle_c(9)
    down.handle(1)

    def ring_far():
        wait(xr.at[0], x_r.at[0])
        x = acc[0] + decode(xr.at[0], ROWS)
        encode(x[:HALF_ROWS], zs_half.at[0])
        encode(x[HALF_ROWS:], zs_half.at[1])
        send(zs_half.at[0], zr_half.at[0], z_s.at[0], z_r.at[0], z_up)
        send(zs_half.at[1], zr_half.at[1], z_s.at[1], z_r.at[1], z_down)

    def ring(k):
        wait(xr.at[k], x_r.at[k])
        side = 1 - k % 2
        x = acc[k] + decode(xr.at[k], ROWS)
        if k < 3:
            wait(zr_half.at[side], z_r.at[side])
            got = decode(zr_half.at[side], HALF_ROWS)
            if side == 0:
                acc[k, 0:HALF_ROWS, :] = x[:HALF_ROWS] + got
                acc[k, HALF_ROWS:ROWS, :] = x[HALF_ROWS:]
            else:
                acc[k, 0:HALF_ROWS, :] = x[:HALF_ROWS]
                acc[k, HALF_ROWS:ROWS, :] = x[HALF_ROWS:] + got
            x = acc[k]
        else:
            wait(zr.at[k - 3], z_r.at[k - 1])
            x = x + decode(zr.at[k - 3], ROWS)
        encode(x, zs.at[k - 1])
        send(zs.at[k - 1], zr.at[k - 1], z_s.at[k + 1], z_r.at[k + 1], z_up if side == 0 else z_down)

    reduce_mid(recv_b, tot_b, 0, 0.5)
    ring_far()
    handle_c(6)
    handle_c(2)
    down.handle(7)
    down.handle(3)
    ring(1)
    ring(2)

    reduce_end(tot_b, half_b, 0)

    def scattered(half, b):
        return jnp.concatenate(
            [jnp.where(pairs[r] == b, half[run_rows(r), :], jnp.zeros((RUN, LANES), BF16)) for r in range(RUNS)],
            axis=0,
        )

    def order_y(m):
        j = m // 2
        return (j == 0) * 2 + (j == 1) * 1 + (j == 2) * 3

    def grad_out(m, carry):
        x = nn(tok_t[...], scattered(half_b, gi(order_y(m), m % 2, 1)))
        encode(x, gcs.at[m])
        send(gcs.at[m], gcr.at[m], gc_s.at[m], gc_r.at[m], core_peer)
        return carry

    lax.fori_loop(0, 8, grad_out, 0)
    handle_c(14)
    handle_c(10)
    handle_c(5)
    handle_c(3)

    def grad_own(m, carry):
        gacc[m] = nn(tok_t[...], scattered(half_b, gi(order_y(m), m % 2, 0)))
        return carry

    lax.fori_loop(0, 8, grad_own, 0)

    down.handle(4)
    down.handle(5)
    ring(3)
    ring(4)

    def grad_sum(m):
        wait(gcr.at[m], gc_r.at[m])
        return gacc[m] + decode(gcr.at[m], WIDTH)

    def grad_send(x, i, to):
        encode(x, gys.at[i])
        send(gys.at[i], gyr.at[i], gy_s.at[i], gy_r.at[i], to)

    def grad_got(i):
        wait(gyr.at[i], gy_r.at[i])
        return decode(gyr.at[i], WIDTH)

    grad_send(grad_sum(0), 0, y_up)
    grad_send(grad_sum(1), 1, y_down)
    grad_send(grad_sum(3), 3, y_up)
    grad_send(grad_sum(4), 4, y_down)

    handle_c(13)
    handle_c(11)
    loads[4].wait()
    for index in range(8, 16):
        down.got(index)
    pack(lambda r: nn(tok[run_rows(r), :], dfull[pairs[r]]), part_d)
    reduce_start(part_d, recv_d, 1)
    ring(5)
    ring(6)

    grad_send(grad_sum(2) + grad_got(0), 2, y_up)
    grad_send(grad_sum(5) + grad_got(1), 5, y_down)

    reduce_mid(recv_d, tot_d, 1, 1.0)

    handle_c(4)
    handle_c(12)
    loads[5].wait()

    def tg_part(n, carry):
        rows = pl.ds(pl.multiple_of(n * 256, 256), 256)
        frozen = nt(cotf[...], kv[rows, :])
        for r in range(RUNS):
            x = frozen[run_rows(r)] + nt(half_b[run_rows(r), :], dfull[pairs[r], rows, :])
            tg[run_rows(r), rows] = x.astype(BF16)
        return carry

    lax.fori_loop(0, WIDTH // 256, tg_part, 0)
    tg_out = pltpu.make_async_copy(tg, tg_h, out_sem.at[0])
    tg_out.start()

    wait(xr.at[7], x_r.at[7])
    reduce_end(tot_d, half_d, 1)

    def up_block(b):
        return 0.5 * nn(cot_t[...], scattered(half_d, b))

    def up_out(m, carry):
        ucs[m] = up_block(gi(order_y(m), m % 2, 1))
        return carry

    lax.fori_loop(0, 8, up_out, 0)
    send(ucs, ucr, uc_s, uc_r, core_peer)

    def up_own(m, carry):
        uacc[m] = up_block(gi(order_y(m), m % 2, 0))
        return carry

    lax.fori_loop(0, 8, up_own, 0)

    wait(zr.at[4], z_r.at[6])
    wait(zr.at[5], z_r.at[7])
    acc[7] = acc[7] + decode(xr.at[7], ROWS) + decode(zr.at[4], ROWS) + decode(zr.at[5], ROWS)
    for r in range(RUNS):
        lifted = nn(half_d[run_rows(r), :], ufull[pairs[r]])
        kvo[run_rows(r), :] = (acc[7, run_rows(r), :] + 0.5 * lifted).astype(BF16)
    kvo_out = pltpu.make_async_copy(kvo, kvo_h, out_sem.at[1])
    kvo_out.start()

    wait(ucr, uc_r)
    uacc[...] = uacc[...] + ucr[...]
    for i, m in enumerate((0, 1, 2, 3, 4, 5, 7)):
        dy, dx = Y_ORDER[m]
        send(uacc.at[m], udr.at[i], ud_s.at[i], ud_r.at[i], (gi(dy, dx, 0), t))

    x = grad_sum(7) + grad_got(3) + grad_got(5)
    encode(x, gxs)
    send(gxs, gxr, gx_s, gx_r, x_peer_g)
    dg[...] = grad_sum(6) + grad_got(2) + grad_got(4)

    total = uacc[6]
    for i in range(7):
        wait(udr.at[i], ud_r.at[i])
        total = total + udr[i]
    ug[...] = total.T
    ug_out = pltpu.make_async_copy(ug, ug_h, out_sem.at[2])
    ug_out.start()

    wait(gxr, gx_r)
    dg[...] = dg[...] + decode(gxr, WIDTH)
    dg_out = pltpu.make_async_copy(dg, dg_h, out_sem.at[3])
    dg_out.start()

    up.drain()
    down.drain()
    for i in range(sent_c[0]):
        wait(cot_h, c_s.at[i])
    for k in range(8):
        wait(xs.at[k], x_s.at[k])
        wait(gcs.at[k], gc_s.at[k])
    wait(zs_half.at[0], z_s.at[0])
    wait(zs_half.at[1], z_s.at[1])
    for k in range(6):
        wait(zs.at[k], z_s.at[k + 2])
        wait(gys.at[k], gy_s.at[k])
    for n, (part, tot) in enumerate(((part_b, tot_b), (part_d, tot_d))):
        wait(part.at[0:240, :], p_s.at[2 * n])
        wait(tot.at[0:240, :], p_s.at[2 * n + 1])
    wait(gxs, gx_s)
    wait(ucs, uc_s)
    for i in range(7):
        wait(udr.at[i], ud_s.at[i])
    for copy in (tg_out, kvo_out, ug_out, dg_out):
        copy.wait()


def on_device(tokens, kv_weight, down_factors, up_factors, cotangent, adapter_ids, owner_slot):
    anywhere = pl.BlockSpec(memory_space=pl.ANY)
    scalars = pl.BlockSpec(memory_space=pltpu.SMEM)
    v = pltpu.VMEM
    i16 = jnp.int16
    dma = pltpu.SemaphoreType.DMA
    shape = jax.ShapeDtypeStruct
    return pl.pallas_call(
        kernel,
        out_shape=(
            shape((ROWS, LANES), BF16),
            shape((ROWS, WIDTH), BF16),
            shape((WIDTH, LANES), F32),
            shape((LANES, LANES), F32),
        ),
        in_specs=[scalars] * 2 + [anywhere] * 5,
        out_specs=(anywhere,) * 4,
        scratch_shapes=[
            v((ROWS, WIDTH), BF16),
            v((WIDTH, COLS), BF16),
            v((ROWS, LANES), BF16),
            v((ROWS, COLS), BF16),
            v((16, WIDTH, LANES), BF16),
            v((16, LANES, LANES), BF16),
            v((WIDTH, ROWS), BF16),
            v((LANES, ROWS), BF16),
            v((8, ROWS, LANES), F32),
            v((8, ROWS + EXTRA, LANES), i16),
            v((8, ROWS + EXTRA, LANES), i16),
            v((2, HALF_ROWS + EXTRA, LANES), i16),
            v((2, HALF_ROWS + EXTRA, LANES), i16),
            v((6, ROWS + EXTRA, LANES), i16),
            v((6, ROWS + EXTRA, LANES), i16),
            v((256, LANES), F32),
            v((16, 16, LANES), F32),
            v((256, LANES), BF16),
            v((256, LANES), F32),
            v((16, 16, LANES), F32),
            v((256, LANES), BF16),
            v((ROWS, LANES), BF16),
            v((ROWS, LANES), BF16),
            v((8, WIDTH, LANES), F32),
            v((8, WIDTH + EXTRA, LANES), i16),
            v((8, WIDTH + EXTRA, LANES), i16),
            v((6, WIDTH + EXTRA, LANES), i16),
            v((6, WIDTH + EXTRA, LANES), i16),
            v((WIDTH + EXTRA, LANES), i16),
            v((WIDTH + EXTRA, LANES), i16),
            v((8, LANES, LANES), F32),
            v((8, LANES, LANES), F32),
            v((8, LANES, LANES), F32),
            v((7, LANES, LANES), F32),
            v((ROWS, LANES), BF16),
            v((ROWS, WIDTH), BF16),
            v((WIDTH, LANES), F32),
            v((LANES, LANES), F32),
            dma((6,)),
            dma((4,)),
            dma((15,)),
            dma((16,)),
            dma((15,)),
            dma((16,)),
            dma((15,)),
            dma((16,)),
            dma((8,)),
            dma((8,)),
            dma((8,)),
            dma((8,)),
            dma((4,)),
            dma((4,)),
            dma((8,)),
            dma((8,)),
            dma((6,)),
            dma((6,)),
            dma,
            dma,
            dma,
            dma,
            dma((7,)),
            dma((7,)),
        ],
        compiler_params=pltpu.CompilerParams(
            collective_id=0, has_side_effects=True, vmem_limit_bytes=56 * 1024 * 1024
        ),
    )(adapter_ids, owner_slot, tokens, kv_weight, down_factors, up_factors, cotangent)


def solution(mesh):
    in_specs = (
        P("grp", "tp"),
        P("tp", None),
        P("tp", "grp"),
        P("grp", "tp"),
        P("grp", "tp"),
        P("grp"),
        P(),
    )
    out_specs = (P("grp", "tp"), P("grp", "tp"), P("tp", "grp"), P("grp", "tp"))
    return jax.shard_map(
        on_device, mesh=mesh, in_specs=in_specs, out_specs=out_specs, check_vma=False
    )
```

```python
import jax
import jax.numpy as jnp
from jax import lax
from jax.experimental import pallas as pl
from jax.experimental.pallas import tpu as pltpu
from jax.sharding import PartitionSpec as P

MESH = pl.DeviceIdType.MESH
F32 = jnp.float32
BF16 = jnp.bfloat16
ROWS = 512
WIDTH = 1024
COLS = 2048
LANES = 128
RUN = 64
RUNS = 8
ZN = 8
YN = 4
EXTRA = 16
LEVELS = 32000.0
HALF_ROWS = ROWS // 2
HALF_WIDTH = WIDTH // 2
Y_ORDER = ((2, 0), (2, 1), (1, 0), (1, 1), (3, 0), (3, 1), (0, 0), (0, 1))


def nt(a, b):
    return lax.dot_general(a, b, (((1,), (1,)), ((), ())), preferred_element_type=F32)


def nn(a, b):
    return jnp.dot(a, b, preferred_element_type=F32)


def encode(x, ref):
    rows = x.shape[0]
    top = jnp.maximum(jnp.max(jnp.abs(x), axis=0, keepdims=True), 1e-30)
    exponent = jnp.ceil(jnp.log2(top) + 1e-4)
    scaled = x * (jnp.exp2(-exponent) * LEVELS)
    ref[0:rows, :] = jnp.round(scaled).astype(jnp.int32).astype(jnp.int16)
    ref[rows : rows + EXTRA, :] = jnp.broadcast_to(
        exponent.astype(jnp.int32), (EXTRA, LANES)
    ).astype(jnp.int16)


def decode(ref, rows):
    exponent = ref[rows : rows + EXTRA, :].astype(jnp.int32).astype(F32)[0:1]
    scale = jnp.exp2(exponent) * (1.0 / LEVELS)
    return ref[0:rows, :].astype(jnp.int32).astype(F32) * scale


def kernel(
    ids,
    owner,
    tok_h,
    kv_h,
    df_h,
    uf_h,
    cot_h,
    kvo_h,
    tg_h,
    dg_h,
    ug_h,
    tok,
    kv,
    cot,
    cotf,
    dfull,
    ufull,
    tok_t,
    cot_t,
    acc,
    xs,
    xr,
    zs_half,
    zr_half,
    zs,
    zr,
    part_b,
    recv_b,
    tot_b,
    part_d,
    recv_d,
    tot_d,
    half_b,
    half_d,
    gacc,
    gcs,
    gcr,
    gys,
    gyr,
    gxs,
    gxr,
    uacc,
    ucs,
    ucr,
    uds,
    udr,
    kvo,
    tg,
    dg,
    ug,
    load_sem,
    out_sem,
    u_s,
    u_r,
    da_s,
    da_r,
    db_s,
    db_r,
    c_s,
    c_r,
    x_s,
    x_r,
    z_s,
    z_r,
    p_s,
    p_r,
    gc_s,
    gc_r,
    gy_s,
    gy_r,
    gx_s,
    gx_r,
    uc_s,
    uc_r,
    ud_s,
    ud_r,
):
    g = lax.axis_index("grp")
    t = lax.axis_index("tp")
    y, xh, c = g // 4, (g // 2) % 2, g % 2
    xl, z = t // ZN, t % ZN

    def gi(dy, dx, dc):
        return ((y + dy) % YN) * 4 + ((xh + dx) % 2) * 2 + (c + dc) % 2

    def ti(dx, dz):
        return ((xl + dx) % 2) * ZN + (z + dz) % ZN

    def send(src, dst, ssem, rsem, to):
        pltpu.make_async_remote_copy(
            src_ref=src, dst_ref=dst, send_sem=ssem, recv_sem=rsem, device_id=to, device_id_type=MESH
        ).start()

    def wait(ref, sem):
        pltpu.make_async_copy(ref, ref, sem).wait()

    def cols(i):
        return pl.ds(pl.multiple_of(i * LANES, LANES), LANES)

    loads = [
        pltpu.make_async_copy(uf_h, ufull.at[g], load_sem.at[0]),
        pltpu.make_async_copy(cot_h, cot, load_sem.at[1]),
        pltpu.make_async_copy(tok_h, tok, load_sem.at[2]),
        pltpu.make_async_copy(kv_h, kv, load_sem.at[3]),
        pltpu.make_async_copy(df_h, dfull.at[g], load_sem.at[4]),
        pltpu.make_async_copy(cot_h, cotf.at[:, cols(t)], load_sem.at[5]),
    ]
    for copy in loads:
        copy.start()

    barrier = pltpu.get_barrier_semaphore()
    for k in range(1, 16):
        pl.semaphore_signal(barrier, inc=1, device_id=(g, (t + k) % 16), device_id_type=MESH)
    for dy, dx in Y_ORDER[:-2] + ((0, 1),):
        pl.semaphore_signal(barrier, inc=1, device_id=(gi(dy, dx, 0), t), device_id_type=MESH)
    pl.semaphore_signal(barrier, inc=1, device_id=(gi(0, 0, 1), t), device_id_type=MESH)
    pl.semaphore_wait(barrier, 15 + 7 + 1)

    x_peer_g = (gi(0, 1, 0), t)
    core_peer = (gi(0, 0, 1), t)
    y_up, y_down = (gi(1, 0, 0), t), (gi(3, 0, 0), t)
    x_peer_t = (g, ti(1, 0))
    z_up, z_down = (g, ti(0, 1)), (g, ti(0, 7))

    class Gather:
        def __init__(self, own, full, rows, ssem, rsem):
            self.rows, self.full, self.ssem, self.rsem, self.sent = rows, full, ssem, rsem, 0
            self.own = own.at[rows, :]

        def slot(self, index):
            return gi((index // 2) % 4, index % 2, index // 8)

        def part(self, index):
            return self.full.at[self.slot(index), self.rows, :]

        def push(self, origin, to, index):
            dst = self.part(origin)
            src = self.own if origin == 0 else dst
            send(src, dst, self.ssem.at[self.sent], self.rsem.at[index], to)
            self.sent += 1

        def begin_straight(self):
            for dy, dx in ((0, 1), (2, 1), (2, 0), (1, 1), (3, 1), (1, 0), (3, 0)):
                self.push(0, (gi(dy, dx, 0), t), ((4 - dy) % 4) * 2 + dx)
            self.push(0, core_peer, 8)

        def begin(self):
            self.push(0, x_peer_g, 1)
            self.push(0, y_up, 6)
            self.push(0, y_down, 2)
            self.push(0, core_peer, 8)

        def got(self, index):
            wait(self.part(index), self.rsem.at[index])

        def to_core(self, index):
            self.got(index)
            self.push(index, core_peer, 8 + index)

        def handle(self, index, upward):
            self.got(index)
            if index == 1:
                self.push(index, y_up, 7)
                self.push(index, y_down, 3)
            if index in (6, 7) and upward:
                self.push(index, y_up, index - 2)
            if index in (2, 3) and not upward:
                self.push(index, y_down, index + 2)
            self.push(index, core_peer, 8 + index)

        def drain(self):
            for i in range(self.sent):
                wait(self.own, self.ssem.at[i])

    up = Gather(uf_h, ufull, pl.ds(0, LANES), u_s, u_r)
    down_a = Gather(df_h, dfull, pl.ds(0, HALF_WIDTH), da_s, da_r)
    down_b = Gather(df_h, dfull, pl.ds(HALF_WIDTH, HALF_WIDTH), db_s, db_r)

    def down(index):
        down_a.handle(index, True)
        down_b.handle(index, False)

    sent_c = [0]

    def push_c(origin, to, index, src=None):
        dst = cotf.at[:, cols(origin)]
        send(dst if src is None else src, dst, c_s.at[sent_c[0]], c_r.at[index], to)
        sent_c[0] += 1

    def handle_c(index):
        dx, dz = index // 8, index % 8
        origin = ti(dx, dz)
        wait(cotf.at[:, cols(origin)], c_r.at[index])
        if index == 8:
            push_c(origin, z_up, 15)
            push_c(origin, z_down, 9)
        elif dz in (7, 6) or (dz == 5 and dx == 0):
            push_c(origin, z_up, index - 1)
        elif dz in (1, 2) or (dz == 3 and dx == 1):
            push_c(origin, z_down, index + 1)

    up.begin_straight()
    push_c(t, z_up, 7, cot_h)
    push_c(t, z_down, 1, cot_h)
    down_a.begin()
    down_b.begin()

    def dz_of(k):
        return (k % 2) * (3 - k // 2) + (1 - k % 2) * (4 + k // 2)

    def base_pair(i, dx):
        weights = [kv[:, cols(ti(dx, dz_of(2 * i + j)))] for j in range(2)]
        x = nn(tok[...], jnp.concatenate(weights, axis=1))
        return x[:, :LANES], x[:, LANES:]

    def base_out(i, carry):
        for j, x in enumerate(base_pair(i, 1)):
            encode(x, xs.at[2 * i + j])
        return carry

    def base_own(i, carry):
        for j, x in enumerate(base_pair(i, 0)):
            acc[2 * i + j] = x
        return carry

    def base_send(*blocks):
        for k in blocks:
            send(xs.at[k], xr.at[k], x_s.at[k], x_r.at[k], x_peer_t)

    loads[2].wait()
    loads[3].wait()
    lax.fori_loop(0, 4, base_out, 0)

    lanes = lax.broadcasted_iota(jnp.int32, (RUN, LANES), 1)
    upper = lanes // RUN
    slots = [owner[ids[r * RUN]] for r in range(RUNS)]
    pairs = [s // 2 for s in slots]
    sides = [s % 2 for s in slots]

    def pack(products, part):
        for q in range(RUNS // 2):
            both = []
            for r in (q, q + RUNS // 2):
                x = jnp.where(upper == sides[r], products(r), 0.0)
                both.append(x + pltpu.roll(x, RUN, 1))
            part[q * RUN : (q + 1) * RUN, :] = jnp.where(upper == 0, both[0], both[1])

    def reduce_start(part, recv, n):
        def body(k, carry):
            peer = (t + k) % 16
            rows = pl.ds(pl.multiple_of(peer * 16, 16), 16)
            send(part.at[rows, :], recv.at[t], p_s.at[2 * n], p_r.at[2 * n], (g, peer))
            return carry

        lax.fori_loop(1, 16, body, 0)
        recv[t] = part[pl.ds(pl.multiple_of(t * 16, 16), 16), :]

    def reduce_mid(recv, tot, n, scale):
        wait(recv.at[0:15], p_r.at[2 * n])
        rows = pl.ds(pl.multiple_of(t * 16, 16), 16)
        tot[rows, :] = (scale * jnp.sum(recv[...], axis=0)).astype(BF16)

        def body(k, carry):
            send(tot.at[rows, :], tot.at[rows, :], p_s.at[2 * n + 1], p_r.at[2 * n + 1], (g, (t + k) % 16))
            return carry

        lax.fori_loop(1, 16, body, 0)

    def reduce_end(tot, half, n):
        wait(tot.at[0:240, :], p_r.at[2 * n + 1])
        for q in range(RUNS // 2):
            both = tot[q * RUN : (q + 1) * RUN, :].astype(F32)
            for side, r in ((0, q), (1, q + RUNS // 2)):
                x = jnp.where(upper == side, both, 0.0)
                x = x + pltpu.roll(x, RUN, 1)
                half[r * RUN : (r + 1) * RUN, :] = jnp.where(upper == sides[r], x, 0.0).astype(BF16)

    def run_rows(r):
        return slice(r * RUN, (r + 1) * RUN)

    def ring_far():
        wait(xr.at[0], x_r.at[0])
        x = acc[0] + decode(xr.at[0], ROWS)
        encode(x[:HALF_ROWS], zs_half.at[0])
        encode(x[HALF_ROWS:], zs_half.at[1])
        send(zs_half.at[0], zr_half.at[0], z_s.at[0], z_r.at[0], z_up)
        send(zs_half.at[1], zr_half.at[1], z_s.at[1], z_r.at[1], z_down)

    def ring(k):
        wait(xr.at[k], x_r.at[k])
        side = 1 - k % 2
        x = acc[k] + decode(xr.at[k], ROWS)
        if k < 3:
            wait(zr_half.at[side], z_r.at[side])
            got = decode(zr_half.at[side], HALF_ROWS)
            if side == 0:
                acc[k, 0:HALF_ROWS, :] = x[:HALF_ROWS] + got
                acc[k, HALF_ROWS:ROWS, :] = x[HALF_ROWS:]
            else:
                acc[k, 0:HALF_ROWS, :] = x[:HALF_ROWS]
                acc[k, HALF_ROWS:ROWS, :] = x[HALF_ROWS:] + got
            x = acc[k]
        else:
            wait(zr.at[k - 3], z_r.at[k - 1])
            x = x + decode(zr.at[k - 3], ROWS)
        encode(x, zs.at[k - 1])
        send(zs.at[k - 1], zr.at[k - 1], z_s.at[k + 1], z_r.at[k + 1], z_up if side == 0 else z_down)

    def scattered(half, b):
        return jnp.concatenate(
            [jnp.where(pairs[r] == b, half[run_rows(r), :], jnp.zeros((RUN, LANES), BF16)) for r in range(RUNS)],
            axis=0,
        )

    def order_y(m):
        j = m // 2
        return (j == 0) * 2 + (j == 1) * 1 + (j == 2) * 3

    def grad_pair(m, dc):
        weights = [scattered(half_b, gi(order_y(2 * m), dx, dc)) for dx in range(2)]
        x = nn(tok_t[...], jnp.concatenate(weights, axis=1))
        return x[:, :LANES], x[:, LANES:]

    def grad_out(m, carry):
        for dx, x in enumerate(grad_pair(m, 1)):
            encode(x, gcs.at[2 * m + dx])
        pair = pl.ds(2 * m, 2)
        send(gcs.at[pair], gcr.at[pair], gc_s.at[m], gc_r.at[m], core_peer)
        return carry

    def grad_own(m, carry):
        for dx, x in enumerate(grad_pair(m, 0)):
            gacc[2 * m + dx] = x
        return carry

    def grad_core(m):
        pair = pl.ds(2 * m, 2)
        wait(gcr.at[pair], gc_r.at[m])

    def grad_sum(m):
        return gacc[m] + decode(gcr.at[m], WIDTH)

    def grad_send(x, i, to):
        encode(x, gys.at[i])
        send(gys.at[i], gyr.at[i], gy_s.at[i], gy_r.at[i], to)

    def grad_got(i):
        wait(gyr.at[i], gy_r.at[i])
        return decode(gyr.at[i], WIDTH)

    def tg_part(n, carry):
        rows = pl.ds(pl.multiple_of(n * 256, 256), 256)
        frozen = nt(cotf[...], kv[rows, :])
        for r in range(RUNS):
            x = frozen[run_rows(r)] + nt(half_b[run_rows(r), :], dfull[pairs[r], rows, :])
            tg[run_rows(r), rows] = x.astype(BF16)
        return carry

    def up_pair(m, dc):
        weights = [scattered(half_d, gi(order_y(2 * m), dx, dc)) for dx in range(2)]
        x = 0.5 * nn(cot_t[...], jnp.concatenate(weights, axis=1))
        return x[:, :LANES], x[:, LANES:]

    def up_out(m, carry):
        for dx, x in enumerate(up_pair(m, 1)):
            ucs[2 * m + dx] = x
        return carry

    def up_own(m, carry):
        for dx, x in enumerate(up_pair(m, 0)):
            uacc[2 * m + dx] = x
        return carry

    for index in (6, 2, 7, 3, 1, 4, 5):
        up.to_core(index)
    loads[0].wait()
    loads[1].wait()
    for index in range(8, 16):
        up.got(index)
    pack(lambda r: nt(cot[run_rows(r), :], ufull[pairs[r]]), part_b)
    reduce_start(part_b, recv_b, 0)
    push_c(t, x_peer_t, 8, cot_h)
    base_send(0)
    handle_c(7)
    handle_c(1)
    down(6)
    down(2)
    lax.fori_loop(0, 4, base_own, 0)
    tok_t[...] = tok[...].T
    cot_t[...] = cot[...].T

    reduce_mid(recv_b, tot_b, 0, 0.5)
    base_send(1, 2)
    handle_c(6)
    handle_c(2)
    down(1)
    handle_c(8)
    ring_far()
    handle_c(5)
    handle_c(3)

    reduce_end(tot_b, half_b, 0)
    lax.fori_loop(0, 4, grad_out, 0)
    down(7)
    down(3)
    lax.fori_loop(0, 4, grad_own, 0)
    grad_core(0)
    grad_send(grad_sum(0), 0, y_up)
    grad_send(grad_sum(1), 1, y_down)
    grad_core(1)
    grad_send(grad_sum(3), 3, y_up)
    grad_core(2)
    grad_send(grad_sum(4), 4, y_down)

    down(4)
    down(5)
    loads[4].wait()
    for index in range(8, 16):
        down_a.got(index)
        down_b.got(index)
    pack(lambda r: nn(tok[run_rows(r), :], dfull[pairs[r]]), part_d)
    reduce_start(part_d, recv_d, 1)
    base_send(3, 4)
    handle_c(15)
    handle_c(9)
    ring(1)
    ring(2)
    grad_send(grad_sum(2) + grad_got(0), 2, y_up)
    grad_send(grad_sum(5) + grad_got(1), 5, y_down)

    reduce_mid(recv_d, tot_d, 1, 1.0)
    base_send(5, 6, 7)
    handle_c(14)
    handle_c(10)
    ring(3)
    ring(4)
    handle_c(13)
    handle_c(11)

    reduce_end(tot_d, half_d, 1)
    lax.fori_loop(0, 4, up_out, 0)
    send(ucs, ucr, uc_s, uc_r, core_peer)
    lax.fori_loop(0, 4, up_own, 0)
    ring(5)
    ring(6)
    wait(ucr, uc_r)
    uacc[...] = uacc[...] + ucr[...]
    for i, m in enumerate((0, 1, 2, 3, 4, 5, 7)):
        dy, dx = Y_ORDER[m]
        encode(uacc[m], uds.at[i])
        send(uds.at[i], udr.at[i], ud_s.at[i], ud_r.at[i], (gi(dy, dx, 0), t))

    handle_c(4)
    handle_c(12)
    loads[5].wait()
    lax.fori_loop(0, WIDTH // 256, tg_part, 0)
    tg_out = pltpu.make_async_copy(tg, tg_h, out_sem.at[0])
    tg_out.start()

    grad_core(3)
    x = grad_sum(7) + grad_got(3) + grad_got(5)
    encode(x, gxs)
    send(gxs, gxr, gx_s, gx_r, x_peer_g)
    dg[...] = grad_sum(6) + grad_got(2) + grad_got(4)

    wait(xr.at[7], x_r.at[7])
    wait(zr.at[4], z_r.at[6])
    wait(zr.at[5], z_r.at[7])
    acc[7] = acc[7] + decode(xr.at[7], ROWS) + decode(zr.at[4], ROWS) + decode(zr.at[5], ROWS)
    for r in range(RUNS):
        lifted = nn(half_d[run_rows(r), :], ufull[pairs[r]])
        kvo[run_rows(r), :] = (acc[7, run_rows(r), :] + 0.5 * lifted).astype(BF16)
    kvo_out = pltpu.make_async_copy(kvo, kvo_h, out_sem.at[1])
    kvo_out.start()

    total = uacc[6]
    for i in range(7):
        wait(udr.at[i], ud_r.at[i])
        total = total + decode(udr.at[i], LANES)
    ug[...] = total.T
    ug_out = pltpu.make_async_copy(ug, ug_h, out_sem.at[2])
    ug_out.start()

    wait(gxr, gx_r)
    dg[...] = dg[...] + decode(gxr, WIDTH)
    dg_out = pltpu.make_async_copy(dg, dg_h, out_sem.at[3])
    dg_out.start()

    up.drain()
    down_a.drain()
    down_b.drain()
    for i in range(sent_c[0]):
        wait(cot_h, c_s.at[i])
    for k in range(8):
        wait(xs.at[k], x_s.at[k])
    for m in range(4):
        wait(gcs.at[pl.ds(2 * m, 2)], gc_s.at[m])
    wait(zs_half.at[0], z_s.at[0])
    wait(zs_half.at[1], z_s.at[1])
    for k in range(6):
        wait(zs.at[k], z_s.at[k + 2])
        wait(gys.at[k], gy_s.at[k])
    for n, (part, tot) in enumerate(((part_b, tot_b), (part_d, tot_d))):
        wait(part.at[0:240, :], p_s.at[2 * n])
        wait(tot.at[0:240, :], p_s.at[2 * n + 1])
    wait(gxs, gx_s)
    wait(ucs, uc_s)
    for i in range(7):
        wait(uds.at[i], ud_s.at[i])
    for copy in (tg_out, kvo_out, ug_out, dg_out):
        copy.wait()


def hand_over(*refs):
    sources, targets, staged, sem = refs[0:4], refs[4:8], refs[8:12], refs[12]
    pieces = []
    for i in (1, 2, 0, 3):
        rows = staged[i].shape[0]
        step = min(rows, 256)
        pieces += [(i, pl.ds(at, step)) for at in range(0, rows, step)]
    loads = [
        pltpu.make_async_copy(sources[i].at[rows, :], staged[i].at[rows, :], sem.at[0, n])
        for n, (i, rows) in enumerate(pieces)
    ]
    stores = [
        pltpu.make_async_copy(staged[i].at[rows, :], targets[i].at[rows, :], sem.at[1, n])
        for n, (i, rows) in enumerate(pieces)
    ]
    for load in loads:
        load.start()
    for load, store in zip(loads, stores):
        load.wait()
        store.start()
    for store in stores:
        store.wait()


def on_device(tokens, kv_weight, down_factors, up_factors, cotangent, adapter_ids, owner_slot):
    anywhere = pl.BlockSpec(memory_space=pl.ANY)
    scalars = pl.BlockSpec(memory_space=pltpu.SMEM)
    v = pltpu.VMEM
    i16 = jnp.int16
    dma = pltpu.SemaphoreType.DMA
    shape = jax.ShapeDtypeStruct
    out_shape = (
        shape((ROWS, LANES), BF16),
        shape((ROWS, WIDTH), BF16),
        shape((WIDTH, LANES), F32),
        shape((LANES, LANES), F32),
    )
    results = pl.pallas_call(
        kernel,
        out_shape=out_shape,
        in_specs=[scalars] * 2 + [anywhere] * 5,
        out_specs=(anywhere,) * 4,
        scratch_shapes=[
            v((ROWS, WIDTH), BF16),
            v((WIDTH, COLS), BF16),
            v((ROWS, LANES), BF16),
            v((ROWS, COLS), BF16),
            v((16, WIDTH, LANES), BF16),
            v((16, LANES, LANES), BF16),
            v((WIDTH, ROWS), BF16),
            v((LANES, ROWS), BF16),
            v((8, ROWS, LANES), F32),
            v((8, ROWS + EXTRA, LANES), i16),
            v((8, ROWS + EXTRA, LANES), i16),
            v((2, HALF_ROWS + EXTRA, LANES), i16),
            v((2, HALF_ROWS + EXTRA, LANES), i16),
            v((6, ROWS + EXTRA, LANES), i16),
            v((6, ROWS + EXTRA, LANES), i16),
            v((256, LANES), F32),
            v((16, 16, LANES), F32),
            v((256, LANES), BF16),
            v((256, LANES), F32),
            v((16, 16, LANES), F32),
            v((256, LANES), BF16),
            v((ROWS, LANES), BF16),
            v((ROWS, LANES), BF16),
            v((8, WIDTH, LANES), F32),
            v((8, WIDTH + EXTRA, LANES), i16),
            v((8, WIDTH + EXTRA, LANES), i16),
            v((6, WIDTH + EXTRA, LANES), i16),
            v((6, WIDTH + EXTRA, LANES), i16),
            v((WIDTH + EXTRA, LANES), i16),
            v((WIDTH + EXTRA, LANES), i16),
            v((8, LANES, LANES), F32),
            v((8, LANES, LANES), F32),
            v((8, LANES, LANES), F32),
            v((7, LANES + EXTRA, LANES), i16),
            v((7, LANES + EXTRA, LANES), i16),
            v((ROWS, LANES), BF16),
            v((ROWS, WIDTH), BF16),
            v((WIDTH, LANES), F32),
            v((LANES, LANES), F32),
            dma((6,)),
            dma((4,)),
            dma((15,)),
            dma((16,)),
            dma((15,)),
            dma((16,)),
            dma((15,)),
            dma((16,)),
            dma((15,)),
            dma((16,)),
            dma((8,)),
            dma((8,)),
            dma((8,)),
            dma((8,)),
            dma((4,)),
            dma((4,)),
            dma((4,)),
            dma((4,)),
            dma((6,)),
            dma((6,)),
            dma,
            dma,
            dma,
            dma,
            dma((7,)),
            dma((7,)),
        ],
        compiler_params=pltpu.CompilerParams(
            collective_id=0, has_side_effects=True, vmem_limit_bytes=56 * 1024 * 1024
        ),
    )(adapter_ids, owner_slot, tokens, kv_weight, down_factors, up_factors, cotangent)
    return pl.pallas_call(
        hand_over,
        out_shape=out_shape,
        in_specs=[anywhere] * 4,
        out_specs=(anywhere,) * 4,
        scratch_shapes=[v(o.shape, o.dtype) for o in out_shape] + [dma((2, 9))],
        compiler_params=pltpu.CompilerParams(vmem_limit_bytes=56 * 1024 * 1024),
    )(*results)


def solution(mesh):
    in_specs = (
        P("grp", "tp"),
        P("tp", None),
        P("tp", "grp"),
        P("grp", "tp"),
        P("grp", "tp"),
        P("grp"),
        P(),
    )
    out_specs = (P("grp", "tp"), P("grp", "tp"), P("tp", "grp"), P("grp", "tp"))
    return jax.shard_map(
        on_device, mesh=mesh, in_specs=in_specs, out_specs=out_specs, check_vma=False
    )
```

```python
import jax
import jax.numpy as jnp
from jax import lax
from jax.experimental import pallas as pl
from jax.experimental.pallas import tpu as pltpu
from jax.sharding import PartitionSpec as P

MESH = pl.DeviceIdType.MESH
F32 = jnp.float32
BF16 = jnp.bfloat16
ROWS = 512
WIDTH = 1024
COLS = 2048
LANES = 128
RUN = 64
RUNS = 8
ZN = 8
YN = 4
EXTRA = 16
LEVELS = 32000.0
HALF_ROWS = ROWS // 2
HALF_WIDTH = WIDTH // 2
Y_ORDER = ((2, 0), (2, 1), (1, 0), (1, 1), (3, 0), (3, 1), (0, 0), (0, 1))


def nt(a, b):
    return lax.dot_general(a, b, (((1,), (1,)), ((), ())), preferred_element_type=F32)


def nn(a, b):
    return jnp.dot(a, b, preferred_element_type=F32)


def encode(x, ref):
    rows = x.shape[0]
    top = jnp.maximum(jnp.max(jnp.abs(x), axis=0, keepdims=True), 1e-30)
    exponent = jnp.ceil(jnp.log2(top) + 1e-4)
    scaled = x * (jnp.exp2(-exponent) * LEVELS)
    ref[0:rows, :] = jnp.round(scaled).astype(jnp.int32).astype(jnp.int16)
    ref[rows : rows + EXTRA, :] = jnp.broadcast_to(
        exponent.astype(jnp.int32), (EXTRA, LANES)
    ).astype(jnp.int16)


def decode(ref, rows):
    exponent = ref[rows : rows + EXTRA, :].astype(jnp.int32).astype(F32)[0:1]
    scale = jnp.exp2(exponent) * (1.0 / LEVELS)
    return ref[0:rows, :].astype(jnp.int32).astype(F32) * scale


def kernel(
    ids,
    owner,
    tok_h,
    kv_h,
    df_h,
    uf_h,
    cot_h,
    kvo_h,
    tg_h,
    dg_h,
    ug_h,
    tok,
    kv,
    cot,
    cotf,
    dfull,
    ufull,
    tok_t,
    cot_t,
    acc,
    xs,
    xr,
    zs_half,
    zr_half,
    zs,
    zr,
    part_b,
    recv_b,
    tot_b,
    part_d,
    recv_d,
    tot_d,
    half_b,
    half_d,
    gacc,
    gcs,
    gcr,
    gfs,
    gfr,
    gys,
    gyr,
    gxs,
    gxr,
    uacc,
    ucs,
    ucr,
    uds,
    udr,
    kvo,
    tg,
    dg,
    ug,
    load_sem,
    out_sem,
    u_s,
    u_r,
    da_s,
    da_r,
    db_s,
    db_r,
    c_s,
    c_r,
    x_s,
    x_r,
    z_s,
    z_r,
    p_s,
    p_r,
    gc_s,
    gc_r,
    gf_s,
    gf_r,
    gy_s,
    gy_r,
    gx_s,
    gx_r,
    uc_s,
    uc_r,
    ud_s,
    ud_r,
):
    g = lax.axis_index("grp")
    t = lax.axis_index("tp")
    y, xh, c = g // 4, (g // 2) % 2, g % 2
    xl, z = t // ZN, t % ZN

    def gi(dy, dx, dc):
        return ((y + dy) % YN) * 4 + ((xh + dx) % 2) * 2 + (c + dc) % 2

    def ti(dx, dz):
        return ((xl + dx) % 2) * ZN + (z + dz) % ZN

    def send(src, dst, ssem, rsem, to):
        pltpu.make_async_remote_copy(
            src_ref=src, dst_ref=dst, send_sem=ssem, recv_sem=rsem, device_id=to, device_id_type=MESH
        ).start()

    def wait(ref, sem):
        pltpu.make_async_copy(ref, ref, sem).wait()

    def cols(i):
        return pl.ds(pl.multiple_of(i * LANES, LANES), LANES)

    loads = [
        pltpu.make_async_copy(uf_h, ufull.at[g], load_sem.at[0]),
        pltpu.make_async_copy(cot_h, cot, load_sem.at[1]),
        pltpu.make_async_copy(tok_h, tok, load_sem.at[2]),
        pltpu.make_async_copy(kv_h, kv, load_sem.at[3]),
        pltpu.make_async_copy(df_h, dfull.at[g], load_sem.at[4]),
        pltpu.make_async_copy(cot_h, cotf.at[:, cols(t)], load_sem.at[5]),
    ]
    for copy in loads:
        copy.start()

    barrier = pltpu.get_barrier_semaphore()
    for k in range(1, 16):
        pl.semaphore_signal(barrier, inc=1, device_id=(g, (t + k) % 16), device_id_type=MESH)
    for dy, dx in Y_ORDER[:-2] + ((0, 1),):
        pl.semaphore_signal(barrier, inc=1, device_id=(gi(dy, dx, 0), t), device_id_type=MESH)
    pl.semaphore_signal(barrier, inc=1, device_id=(gi(0, 0, 1), t), device_id_type=MESH)
    pl.semaphore_wait(barrier, 15 + 7 + 1)

    x_peer_g = (gi(0, 1, 0), t)
    core_peer = (gi(0, 0, 1), t)
    y_up, y_down = (gi(1, 0, 0), t), (gi(3, 0, 0), t)
    x_peer_t = (g, ti(1, 0))
    z_up, z_down = (g, ti(0, 1)), (g, ti(0, 7))

    class Gather:
        def __init__(self, own, full, rows, ssem, rsem):
            self.rows, self.full, self.ssem, self.rsem, self.sent = rows, full, ssem, rsem, 0
            self.own = own.at[rows, :]

        def slot(self, index):
            return gi((index // 2) % 4, index % 2, index // 8)

        def part(self, index):
            return self.full.at[self.slot(index), self.rows, :]

        def push(self, origin, to, index):
            dst = self.part(origin)
            src = self.own if origin == 0 else dst
            send(src, dst, self.ssem.at[self.sent], self.rsem.at[index], to)
            self.sent += 1

        def begin_straight(self):
            for dy, dx in ((0, 1), (2, 1), (2, 0), (1, 1), (3, 1), (1, 0), (3, 0)):
                self.push(0, (gi(dy, dx, 0), t), ((4 - dy) % 4) * 2 + dx)
            self.push(0, core_peer, 8)

        def begin(self):
            self.push(0, x_peer_g, 1)
            self.push(0, y_up, 6)
            self.push(0, y_down, 2)
            self.push(0, core_peer, 8)

        def got(self, index):
            wait(self.part(index), self.rsem.at[index])

        def to_core(self, index):
            self.got(index)
            self.push(index, core_peer, 8 + index)

        def handle(self, index, upward):
            self.got(index)
            if index == 1:
                self.push(index, y_up, 7)
                self.push(index, y_down, 3)
            if index in (6, 7) and upward:
                self.push(index, y_up, index - 2)
            if index in (2, 3) and not upward:
                self.push(index, y_down, index + 2)
            self.push(index, core_peer, 8 + index)

        def drain(self):
            for i in range(self.sent):
                wait(self.own, self.ssem.at[i])

    up = Gather(uf_h, ufull, pl.ds(0, LANES), u_s, u_r)
    down_a = Gather(df_h, dfull, pl.ds(0, HALF_WIDTH), da_s, da_r)
    down_b = Gather(df_h, dfull, pl.ds(HALF_WIDTH, HALF_WIDTH), db_s, db_r)

    sent_c = [0]

    def push_c(origin, to, index, src=None):
        dst = cotf.at[:, cols(origin)]
        send(dst if src is None else src, dst, c_s.at[sent_c[0]], c_r.at[index], to)
        sent_c[0] += 1

    def handle_c(index):
        dx, dz = index // 8, index % 8
        origin = ti(dx, dz)
        wait(cotf.at[:, cols(origin)], c_r.at[index])
        if index == 8:
            push_c(origin, z_up, 15)
            push_c(origin, z_down, 9)
        elif dz in (7, 6) or (dz == 5 and dx == 0):
            push_c(origin, z_up, index - 1)
        elif dz in (1, 2) or (dz == 3 and dx == 1):
            push_c(origin, z_down, index + 1)

    up.begin_straight()
    push_c(t, z_up, 7, cot_h)
    push_c(t, z_down, 1, cot_h)
    down_a.begin()
    down_b.begin()
    push_c(t, x_peer_t, 8, cot_h)

    def dz_of(k):
        return (k % 2) * (3 - k // 2) + (1 - k % 2) * (4 + k // 2)

    def base_pair(i, dx):
        weights = [kv[:, cols(ti(dx, dz_of(2 * i + j)))] for j in range(2)]
        x = nn(tok[...], jnp.concatenate(weights, axis=1))
        return x[:, :LANES], x[:, LANES:]

    def base_out(i, carry):
        for j, x in enumerate(base_pair(i, 1)):
            encode(x, xs.at[2 * i + j])
        return carry

    def base_own(i, carry):
        for j, x in enumerate(base_pair(i, 0)):
            acc[2 * i + j] = x
        return carry

    def base_send(*blocks):
        for k in blocks:
            send(xs.at[k], xr.at[k], x_s.at[k], x_r.at[k], x_peer_t)

    loads[2].wait()
    loads[3].wait()
    lax.fori_loop(0, 4, base_out, 0)

    lanes = lax.broadcasted_iota(jnp.int32, (RUN, LANES), 1)
    upper = lanes // RUN
    slots = [owner[ids[r * RUN]] for r in range(RUNS)]
    pairs = [s // 2 for s in slots]
    sides = [s % 2 for s in slots]

    def pack(products, part):
        for q in range(RUNS // 2):
            both = []
            for r in (q, q + RUNS // 2):
                x = jnp.where(upper == sides[r], products(r), 0.0)
                both.append(x + pltpu.roll(x, RUN, 1))
            part[q * RUN : (q + 1) * RUN, :] = jnp.where(upper == 0, both[0], both[1])

    def reduce_start(part, recv, n):
        def body(k, carry):
            peer = (t + k) % 16
            rows = pl.ds(pl.multiple_of(peer * 16, 16), 16)
            send(part.at[rows, :], recv.at[t], p_s.at[2 * n], p_r.at[2 * n], (g, peer))
            return carry

        lax.fori_loop(1, 16, body, 0)
        recv[t] = part[pl.ds(pl.multiple_of(t * 16, 16), 16), :]

    def reduce_mid(recv, tot, n, scale):
        wait(recv.at[0:15], p_r.at[2 * n])
        rows = pl.ds(pl.multiple_of(t * 16, 16), 16)
        tot[rows, :] = (scale * jnp.sum(recv[...], axis=0)).astype(BF16)

        def body(k, carry):
            send(tot.at[rows, :], tot.at[rows, :], p_s.at[2 * n + 1], p_r.at[2 * n + 1], (g, (t + k) % 16))
            return carry

        lax.fori_loop(1, 16, body, 0)

    def reduce_end(tot, half, n):
        wait(tot.at[0:240, :], p_r.at[2 * n + 1])
        for q in range(RUNS // 2):
            both = tot[q * RUN : (q + 1) * RUN, :].astype(F32)
            for side, r in ((0, q), (1, q + RUNS // 2)):
                x = jnp.where(upper == side, both, 0.0)
                x = x + pltpu.roll(x, RUN, 1)
                half[r * RUN : (r + 1) * RUN, :] = jnp.where(upper == sides[r], x, 0.0).astype(BF16)

    def run_rows(r):
        return slice(r * RUN, (r + 1) * RUN)

    def ring_far():
        wait(xr.at[0], x_r.at[0])
        x = acc[0] + decode(xr.at[0], ROWS)
        encode(x[:HALF_ROWS], zs_half.at[0])
        encode(x[HALF_ROWS:], zs_half.at[1])
        send(zs_half.at[0], zr_half.at[0], z_s.at[0], z_r.at[0], z_up)
        send(zs_half.at[1], zr_half.at[1], z_s.at[1], z_r.at[1], z_down)

    def ring(k):
        wait(xr.at[k], x_r.at[k])
        side = 1 - k % 2
        x = acc[k] + decode(xr.at[k], ROWS)
        if k < 3:
            wait(zr_half.at[side], z_r.at[side])
            got = decode(zr_half.at[side], HALF_ROWS)
            if side == 0:
                acc[k, 0:HALF_ROWS, :] = x[:HALF_ROWS] + got
                acc[k, HALF_ROWS:ROWS, :] = x[HALF_ROWS:]
            else:
                acc[k, 0:HALF_ROWS, :] = x[:HALF_ROWS]
                acc[k, HALF_ROWS:ROWS, :] = x[HALF_ROWS:] + got
            x = acc[k]
        else:
            wait(zr.at[k - 3], z_r.at[k - 1])
            x = x + decode(zr.at[k - 3], ROWS)
        encode(x, zs.at[k - 1])
        send(zs.at[k - 1], zr.at[k - 1], z_s.at[k + 1], z_r.at[k + 1], z_up if side == 0 else z_down)

    def scattered(half, b):
        return jnp.concatenate(
            [jnp.where(pairs[r] == b, half[run_rows(r), :], jnp.zeros((RUN, LANES), BF16)) for r in range(RUNS)],
            axis=0,
        )

    def order_y(m):
        j = m // 2
        return (j == 0) * 2 + (j == 1) * 1 + (j == 2) * 3

    def grad_pair(m, dc):
        weights = [scattered(half_b, gi(order_y(2 * m), dx, dc)) for dx in range(2)]
        x = nn(tok_t[...], jnp.concatenate(weights, axis=1))
        return x[:, :LANES], x[:, LANES:]

    def grad_out(m, carry):
        for dx, x in enumerate(grad_pair(m, 1)):
            encode(x, gcs.at[2 * m + dx])
        pair = pl.ds(2 * m, 2)
        send(gcs.at[pair], gcr.at[pair], gc_s.at[m], gc_r.at[m], core_peer)
        return carry

    def grad_own(m, carry):
        for dx, x in enumerate(grad_pair(m, 0)):
            gacc[2 * m + dx] = x
        return carry

    def grad_core(m):
        pair = pl.ds(2 * m, 2)
        wait(gcr.at[pair], gc_r.at[m])

    def grad_sum(m):
        return gacc[m] + decode(gcr.at[m], WIDTH)

    def grad_far(dx):
        x = grad_sum(dx)
        for way, to in enumerate((y_up, y_down)):
            i = 2 * way + dx
            encode(x[way * HALF_WIDTH : (way + 1) * HALF_WIDTH], gfs.at[i])
            send(gfs.at[i], gfr.at[i], gf_s.at[i], gf_r.at[i], to)

    def grad_near(way, dx):
        i, m = 2 * way + dx, 2 + 2 * way + dx
        wait(gfr.at[i], gf_r.at[i])
        x = grad_sum(m)
        far = decode(gfr.at[i], HALF_WIDTH)
        parts = [x[:HALF_WIDTH], x[HALF_WIDTH:]]
        parts[way] = parts[way] + far
        encode(jnp.concatenate(parts, axis=0), gys.at[i])
        send(gys.at[i], gyr.at[i], gy_s.at[i], gy_r.at[i], y_down if way else y_up)

    def grad_total(dx):
        wait(gyr.at[dx], gy_r.at[dx])
        wait(gyr.at[2 + dx], gy_r.at[2 + dx])
        return grad_sum(6 + dx) + decode(gyr.at[dx], WIDTH) + decode(gyr.at[2 + dx], WIDTH)

    def tg_part(n, carry):
        rows = pl.ds(pl.multiple_of(n * 256, 256), 256)
        frozen = nt(cotf[...], kv[rows, :])
        for r in range(RUNS):
            x = frozen[run_rows(r)] + nt(half_b[run_rows(r), :], dfull[pairs[r], rows, :])
            tg[run_rows(r), rows] = x.astype(BF16)
        return carry

    def up_pair(m, dc):
        weights = [scattered(half_d, gi(order_y(2 * m), dx, dc)) for dx in range(2)]
        x = 0.5 * nn(cot_t[...], jnp.concatenate(weights, axis=1))
        return x[:, :LANES], x[:, LANES:]

    def up_out(m, carry):
        for dx, x in enumerate(up_pair(m, 1)):
            ucs[2 * m + dx] = x
        return carry

    def up_own(m, carry):
        for dx, x in enumerate(up_pair(m, 0)):
            uacc[2 * m + dx] = x
        return carry

    for index in (6, 2, 1, 7, 3):
        up.to_core(index)
    down_a.handle(6, True)
    down_b.handle(2, False)
    handle_c(7)
    handle_c(1)
    for index in (4, 5):
        up.to_core(index)
    loads[0].wait()
    loads[1].wait()
    for index in range(8, 16):
        up.got(index)
    pack(lambda r: nt(cot[run_rows(r), :], ufull[pairs[r]]), part_b)
    reduce_start(part_b, recv_b, 0)
    base_send(0, 1)
    down_a.handle(1, True)
    handle_c(6)
    handle_c(2)
    lax.fori_loop(0, 4, base_own, 0)
    down_b.handle(1, False)
    handle_c(8)
    down_b.handle(6, False)
    down_a.handle(2, True)
    tok_t[...] = tok[...].T
    cot_t[...] = cot[...].T

    reduce_mid(recv_b, tot_b, 0, 0.5)
    base_send(2, 3, 4, 5)
    down_a.handle(7, True)
    down_b.handle(3, False)
    handle_c(5)
    handle_c(3)
    ring_far()

    reduce_end(tot_b, half_b, 0)
    grad_out(0, 0)
    grad_own(0, 0)
    grad_out(1, 0)
    grad_core(0)
    grad_far(1)
    grad_far(0)
    handle_c(15)
    handle_c(9)
    grad_own(1, 0)
    lax.fori_loop(2, 4, grad_out, 0)
    lax.fori_loop(2, 4, grad_own, 0)
    down_b.handle(7, False)
    down_a.handle(3, True)
    for half_gather, upward in ((down_a, True), (down_b, False)):
        half_gather.handle(4, upward)
        half_gather.handle(5, upward)
    loads[4].wait()
    for index in range(8, 16):
        down_a.got(index)
        down_b.got(index)
    pack(lambda r: nn(tok[run_rows(r), :], dfull[pairs[r]]), part_d)
    reduce_start(part_d, recv_d, 1)
    base_send(6, 7)
    grad_core(1)
    grad_core(2)
    grad_near(0, 1)
    grad_near(1, 1)
    handle_c(14)
    handle_c(10)
    grad_near(0, 0)
    grad_near(1, 0)
    ring(1)
    ring(2)

    reduce_mid(recv_d, tot_d, 1, 1.0)
    handle_c(13)
    handle_c(11)
    ring(3)
    ring(4)
    grad_core(3)
    encode(grad_total(1), gxs)
    send(gxs, gxr, gx_s, gx_r, x_peer_g)

    reduce_end(tot_d, half_d, 1)
    lax.fori_loop(0, 4, up_out, 0)
    send(ucs, ucr, uc_s, uc_r, core_peer)
    lax.fori_loop(0, 4, up_own, 0)
    ring(5)
    ring(6)
    wait(ucr, uc_r)
    uacc[...] = uacc[...] + ucr[...]
    for i, m in enumerate((0, 1, 2, 3, 4, 5, 7)):
        dy, dx = Y_ORDER[m]
        encode(uacc[m], uds.at[i])
        send(uds.at[i], udr.at[i], ud_s.at[i], ud_r.at[i], (gi(dy, dx, 0), t))

    handle_c(4)
    handle_c(12)
    loads[5].wait()
    lax.fori_loop(0, WIDTH // 256, tg_part, 0)
    tg_out = pltpu.make_async_copy(tg, tg_h, out_sem.at[0])
    tg_out.start()
    dg[...] = grad_total(0)

    wait(xr.at[7], x_r.at[7])
    wait(zr.at[4], z_r.at[6])
    wait(zr.at[5], z_r.at[7])
    acc[7] = acc[7] + decode(xr.at[7], ROWS) + decode(zr.at[4], ROWS) + decode(zr.at[5], ROWS)
    for r in range(RUNS):
        lifted = nn(half_d[run_rows(r), :], ufull[pairs[r]])
        kvo[run_rows(r), :] = (acc[7, run_rows(r), :] + 0.5 * lifted).astype(BF16)
    kvo_out = pltpu.make_async_copy(kvo, kvo_h, out_sem.at[1])
    kvo_out.start()

    wait(gxr, gx_r)
    dg[...] = dg[...] + decode(gxr, WIDTH)
    dg_out = pltpu.make_async_copy(dg, dg_h, out_sem.at[3])
    dg_out.start()

    total = uacc[6]
    for i in range(7):
        wait(udr.at[i], ud_r.at[i])
        total = total + decode(udr.at[i], LANES)
    ug[...] = total.T
    ug_out = pltpu.make_async_copy(ug, ug_h, out_sem.at[2])
    ug_out.start()

    up.drain()
    down_a.drain()
    down_b.drain()
    for i in range(sent_c[0]):
        wait(cot_h, c_s.at[i])
    for k in range(8):
        wait(xs.at[k], x_s.at[k])
    for m in range(4):
        wait(gcs.at[pl.ds(2 * m, 2)], gc_s.at[m])
        wait(gfs.at[m], gf_s.at[m])
        wait(gys.at[m], gy_s.at[m])
    wait(zs_half.at[0], z_s.at[0])
    wait(zs_half.at[1], z_s.at[1])
    for k in range(6):
        wait(zs.at[k], z_s.at[k + 2])
    for n, (part, tot) in enumerate(((part_b, tot_b), (part_d, tot_d))):
        wait(part.at[0:240, :], p_s.at[2 * n])
        wait(tot.at[0:240, :], p_s.at[2 * n + 1])
    wait(gxs, gx_s)
    wait(ucs, uc_s)
    for i in range(7):
        wait(uds.at[i], ud_s.at[i])
    for copy in (tg_out, kvo_out, ug_out, dg_out):
        copy.wait()


def hand_over(*refs):
    sources, targets, staged, sem = refs[0:4], refs[4:8], refs[8:12], refs[12]
    pieces = []
    for i in (1, 2, 0, 3):
        rows = staged[i].shape[0]
        step = min(rows, 256)
        pieces += [(i, pl.ds(at, step)) for at in range(0, rows, step)]
    loads = [
        pltpu.make_async_copy(sources[i].at[rows, :], staged[i].at[rows, :], sem.at[0, n])
        for n, (i, rows) in enumerate(pieces)
    ]
    stores = [
        pltpu.make_async_copy(staged[i].at[rows, :], targets[i].at[rows, :], sem.at[1, n])
        for n, (i, rows) in enumerate(pieces)
    ]
    for load in loads:
        load.start()
    for load, store in zip(loads, stores):
        load.wait()
        store.start()
    for store in stores:
        store.wait()


def on_device(tokens, kv_weight, down_factors, up_factors, cotangent, adapter_ids, owner_slot):
    anywhere = pl.BlockSpec(memory_space=pl.ANY)
    scalars = pl.BlockSpec(memory_space=pltpu.SMEM)
    v = pltpu.VMEM
    i16 = jnp.int16
    dma = pltpu.SemaphoreType.DMA
    shape = jax.ShapeDtypeStruct
    out_shape = (
        shape((ROWS, LANES), BF16),
        shape((ROWS, WIDTH), BF16),
        shape((WIDTH, LANES), F32),
        shape((LANES, LANES), F32),
    )
    results = pl.pallas_call(
        kernel,
        out_shape=out_shape,
        in_specs=[scalars] * 2 + [anywhere] * 5,
        out_specs=(anywhere,) * 4,
        scratch_shapes=[
            v((ROWS, WIDTH), BF16),
            v((WIDTH, COLS), BF16),
            v((ROWS, LANES), BF16),
            v((ROWS, COLS), BF16),
            v((16, WIDTH, LANES), BF16),
            v((16, LANES, LANES), BF16),
            v((WIDTH, ROWS), BF16),
            v((LANES, ROWS), BF16),
            v((8, ROWS, LANES), F32),
            v((8, ROWS + EXTRA, LANES), i16),
            v((8, ROWS + EXTRA, LANES), i16),
            v((2, HALF_ROWS + EXTRA, LANES), i16),
            v((2, HALF_ROWS + EXTRA, LANES), i16),
            v((6, ROWS + EXTRA, LANES), i16),
            v((6, ROWS + EXTRA, LANES), i16),
            v((256, LANES), F32),
            v((16, 16, LANES), F32),
            v((256, LANES), BF16),
            v((256, LANES), F32),
            v((16, 16, LANES), F32),
            v((256, LANES), BF16),
            v((ROWS, LANES), BF16),
            v((ROWS, LANES), BF16),
            v((8, WIDTH, LANES), F32),
            v((8, WIDTH + EXTRA, LANES), i16),
            v((8, WIDTH + EXTRA, LANES), i16),
            v((4, HALF_WIDTH + EXTRA, LANES), i16),
            v((4, HALF_WIDTH + EXTRA, LANES), i16),
            v((4, WIDTH + EXTRA, LANES), i16),
            v((4, WIDTH + EXTRA, LANES), i16),
            v((WIDTH + EXTRA, LANES), i16),
            v((WIDTH + EXTRA, LANES), i16),
            v((8, LANES, LANES), F32),
            v((8, LANES, LANES), F32),
            v((8, LANES, LANES), F32),
            v((7, LANES + EXTRA, LANES), i16),
            v((7, LANES + EXTRA, LANES), i16),
            v((ROWS, LANES), BF16),
            v((ROWS, WIDTH), BF16),
            v((WIDTH, LANES), F32),
            v((LANES, LANES), F32),
            dma((6,)),
            dma((4,)),
            dma((15,)),
            dma((16,)),
            dma((15,)),
            dma((16,)),
            dma((15,)),
            dma((16,)),
            dma((15,)),
            dma((16,)),
            dma((8,)),
            dma((8,)),
            dma((8,)),
            dma((8,)),
            dma((4,)),
            dma((4,)),
            dma((4,)),
            dma((4,)),
            dma((4,)),
            dma((4,)),
            dma((4,)),
            dma((4,)),
            dma,
            dma,
            dma,
            dma,
            dma((7,)),
            dma((7,)),
        ],
        compiler_params=pltpu.CompilerParams(
            collective_id=0, has_side_effects=True, vmem_limit_bytes=56 * 1024 * 1024
        ),
    )(adapter_ids, owner_slot, tokens, kv_weight, down_factors, up_factors, cotangent)
    return pl.pallas_call(
        hand_over,
        out_shape=out_shape,
        in_specs=[anywhere] * 4,
        out_specs=(anywhere,) * 4,
        scratch_shapes=[v(o.shape, o.dtype) for o in out_shape] + [dma((2, 9))],
        compiler_params=pltpu.CompilerParams(vmem_limit_bytes=56 * 1024 * 1024),
    )(*results)


def solution(mesh):
    in_specs = (
        P("grp", "tp"),
        P("tp", None),
        P("tp", "grp"),
        P("grp", "tp"),
        P("grp", "tp"),
        P("grp"),
        P(),
    )
    out_specs = (P("grp", "tp"), P("grp", "tp"), P("tp", "grp"), P("grp", "tp"))
    return jax.shard_map(
        on_device, mesh=mesh, in_specs=in_specs, out_specs=out_specs, check_vma=False
    )
```

```python
import jax
import jax.numpy as jnp
from jax import lax
from jax.experimental import pallas as pl
from jax.experimental.pallas import tpu as pltpu
from jax.sharding import PartitionSpec as P

MESH = pl.DeviceIdType.MESH
F32 = jnp.float32
BF16 = jnp.bfloat16
ROWS = 512
WIDTH = 1024
COLS = 2048
LANES = 128
RUN = 64
RUNS = 8
ZN = 8
YN = 4
EXTRA = 16
LEVELS = 32000.0
HALF_ROWS = ROWS // 2
HALF_WIDTH = WIDTH // 2
Y_ORDER = ((2, 0), (2, 1), (1, 0), (1, 1), (3, 0), (3, 1), (0, 0), (0, 1))


def nt(a, b):
    return lax.dot_general(a, b, (((1,), (1,)), ((), ())), preferred_element_type=F32)


def nn(a, b):
    return jnp.dot(a, b, preferred_element_type=F32)


def encode(x, ref):
    rows = x.shape[0]
    top = jnp.maximum(jnp.max(jnp.abs(x), axis=0, keepdims=True), 1e-30)
    exponent = jnp.ceil(jnp.log2(top) + 1e-4)
    scaled = x * (jnp.exp2(-exponent) * LEVELS)
    ref[0:rows, :] = jnp.round(scaled).astype(jnp.int32).astype(jnp.int16)
    ref[rows : rows + EXTRA, :] = jnp.broadcast_to(
        exponent.astype(jnp.int32), (EXTRA, LANES)
    ).astype(jnp.int16)


def decode(ref, rows):
    exponent = ref[rows : rows + EXTRA, :].astype(jnp.int32).astype(F32)[0:1]
    scale = jnp.exp2(exponent) * (1.0 / LEVELS)
    return ref[0:rows, :].astype(jnp.int32).astype(F32) * scale


def kernel(
    ids,
    owner,
    tok_h,
    kv_h,
    df_h,
    uf_h,
    cot_h,
    kvo_h,
    tg_h,
    dg_h,
    ug_h,
    tok,
    kv,
    cot,
    cotf,
    dfull,
    ufull,
    tok_t,
    cot_t,
    acc,
    xs,
    xr,
    zs_half,
    zr_half,
    zs,
    zr,
    part_b,
    recv_b,
    tot_b,
    part_d,
    recv_d,
    tot_d,
    half_b,
    half_d,
    gacc,
    gcs,
    gcr,
    gfs,
    gfr,
    gys,
    gyr,
    gxs,
    gxr,
    uacc,
    ucs,
    ucr,
    uds,
    udr,
    kvo,
    tg,
    dg,
    ug,
    load_sem,
    out_sem,
    u_s,
    u_r,
    da_s,
    da_r,
    db_s,
    db_r,
    c_s,
    c_r,
    x_s,
    x_r,
    z_s,
    z_r,
    p_s,
    p_r,
    gc_s,
    gc_r,
    gf_s,
    gf_r,
    gy_s,
    gy_r,
    gx_s,
    gx_r,
    uc_s,
    uc_r,
    ud_s,
    ud_r,
):
    g = lax.axis_index("grp")
    t = lax.axis_index("tp")
    y, xh, c = g // 4, (g // 2) % 2, g % 2
    xl, z = t // ZN, t % ZN

    def gi(dy, dx, dc):
        return ((y + dy) % YN) * 4 + ((xh + dx) % 2) * 2 + (c + dc) % 2

    def ti(dx, dz):
        return ((xl + dx) % 2) * ZN + (z + dz) % ZN

    def send(src, dst, ssem, rsem, to):
        pltpu.make_async_remote_copy(
            src_ref=src, dst_ref=dst, send_sem=ssem, recv_sem=rsem, device_id=to, device_id_type=MESH
        ).start()

    def wait(ref, sem):
        pltpu.make_async_copy(ref, ref, sem).wait()

    def cols(i):
        return pl.ds(pl.multiple_of(i * LANES, LANES), LANES)

    loads = [
        pltpu.make_async_copy(uf_h, ufull.at[g], load_sem.at[0]),
        pltpu.make_async_copy(cot_h, cot, load_sem.at[1]),
        pltpu.make_async_copy(tok_h, tok, load_sem.at[2]),
        pltpu.make_async_copy(kv_h, kv, load_sem.at[3]),
        pltpu.make_async_copy(df_h, dfull.at[g], load_sem.at[4]),
        pltpu.make_async_copy(cot_h, cotf.at[:, cols(t)], load_sem.at[5]),
    ]
    for copy in loads:
        copy.start()

    barrier = pltpu.get_barrier_semaphore()
    for k in range(1, 16):
        pl.semaphore_signal(barrier, inc=1, device_id=(g, (t + k) % 16), device_id_type=MESH)
    for dy, dx in Y_ORDER[:-2] + ((0, 1),):
        pl.semaphore_signal(barrier, inc=1, device_id=(gi(dy, dx, 0), t), device_id_type=MESH)
    pl.semaphore_signal(barrier, inc=1, device_id=(gi(0, 0, 1), t), device_id_type=MESH)
    def dz_of(k):
        return (k % 2) * (3 - k // 2) + (1 - k % 2) * (4 + k // 2)

    def base_pair(i, dx):
        weights = [kv[:, cols(ti(dx, dz_of(2 * i + j)))] for j in range(2)]
        x = nn(tok[...], jnp.concatenate(weights, axis=1))
        return x[:, :LANES], x[:, LANES:]

    def base_out(i, carry):
        for j, x in enumerate(base_pair(i, 1)):
            encode(x, xs.at[2 * i + j])
        return carry

    def base_own(i, carry):
        for j, x in enumerate(base_pair(i, 0)):
            acc[2 * i + j] = x
        return carry

    loads[1].wait()
    loads[2].wait()
    loads[3].wait()
    lax.fori_loop(0, 4, base_out, 0)
    pl.semaphore_wait(barrier, 15 + 7 + 1)

    x_peer_g = (gi(0, 1, 0), t)
    core_peer = (gi(0, 0, 1), t)
    y_up, y_down = (gi(1, 0, 0), t), (gi(3, 0, 0), t)
    x_peer_t = (g, ti(1, 0))
    z_up, z_down = (g, ti(0, 1)), (g, ti(0, 7))

    class Gather:
        def __init__(self, own, full, rows, ssem, rsem):
            self.rows, self.full, self.ssem, self.rsem, self.sent = rows, full, ssem, rsem, 0
            self.own = own.at[rows, :]

        def slot(self, index):
            return gi((index // 2) % 4, index % 2, index // 8)

        def part(self, index):
            return self.full.at[self.slot(index), self.rows, :]

        def push(self, origin, to, index):
            dst = self.part(origin)
            src = self.own if origin == 0 else dst
            send(src, dst, self.ssem.at[self.sent], self.rsem.at[index], to)
            self.sent += 1

        def begin_straight(self):
            for dy, dx in ((0, 1), (2, 1), (2, 0), (1, 1), (3, 1), (1, 0), (3, 0)):
                self.push(0, (gi(dy, dx, 0), t), ((4 - dy) % 4) * 2 + dx)
            self.push(0, core_peer, 8)

        def begin(self):
            self.push(0, x_peer_g, 1)
            self.push(0, y_up, 6)
            self.push(0, y_down, 2)
            self.push(0, core_peer, 8)

        def got(self, index):
            wait(self.part(index), self.rsem.at[index])

        def to_core(self, index):
            self.got(index)
            self.push(index, core_peer, 8 + index)

        def handle(self, index, upward):
            self.got(index)
            if index == 1:
                self.push(index, y_up, 7)
                self.push(index, y_down, 3)
            if index in (6, 7) and upward:
                self.push(index, y_up, index - 2)
            if index in (2, 3) and not upward:
                self.push(index, y_down, index + 2)
            self.push(index, core_peer, 8 + index)

        def drain(self):
            for i in range(self.sent):
                wait(self.own, self.ssem.at[i])

    up = Gather(uf_h, ufull, pl.ds(0, LANES), u_s, u_r)
    down_a = Gather(df_h, dfull, pl.ds(0, HALF_WIDTH), da_s, da_r)
    down_b = Gather(df_h, dfull, pl.ds(HALF_WIDTH, HALF_WIDTH), db_s, db_r)

    sent_c = [0]

    def push_c(origin, to, index, src=None):
        dst = cotf.at[:, cols(origin)]
        send(dst if src is None else src, dst, c_s.at[sent_c[0]], c_r.at[index], to)
        sent_c[0] += 1

    def handle_c(index):
        dx, dz = index // 8, index % 8
        origin = ti(dx, dz)
        wait(cotf.at[:, cols(origin)], c_r.at[index])
        if index == 8:
            push_c(origin, z_up, 15)
            push_c(origin, z_down, 9)
        elif dz in (7, 6) or (dz == 5 and dx == 0):
            push_c(origin, z_up, index - 1)
        elif dz in (1, 2) or (dz == 3 and dx == 1):
            push_c(origin, z_down, index + 1)

    up.begin_straight()
    push_c(t, z_up, 7, cot_h)
    push_c(t, z_down, 1, cot_h)
    down_a.begin()
    down_b.begin()
    push_c(t, x_peer_t, 8, cot_h)

    def base_send(*blocks):
        for k in blocks:
            send(xs.at[k], xr.at[k], x_s.at[k], x_r.at[k], x_peer_t)

    lax.fori_loop(0, 4, base_own, 0)
    tok_t[...] = tok[...].T
    cot_t[...] = cot[...].T

    lanes = lax.broadcasted_iota(jnp.int32, (RUN, LANES), 1)
    upper = lanes // RUN
    slots = [owner[ids[r * RUN]] for r in range(RUNS)]
    pairs = [s // 2 for s in slots]
    sides = [s % 2 for s in slots]

    def pack(products, part):
        for q in range(RUNS // 2):
            both = []
            for r in (q, q + RUNS // 2):
                x = jnp.where(upper == sides[r], products(r), 0.0)
                both.append(x + pltpu.roll(x, RUN, 1))
            part[q * RUN : (q + 1) * RUN, :] = jnp.where(upper == 0, both[0], both[1])

    def reduce_start(part, recv, n):
        def body(k, carry):
            peer = (t + k) % 16
            rows = pl.ds(pl.multiple_of(peer * 16, 16), 16)
            send(part.at[rows, :], recv.at[t], p_s.at[2 * n], p_r.at[2 * n], (g, peer))
            return carry

        lax.fori_loop(1, 16, body, 0)
        recv[t] = part[pl.ds(pl.multiple_of(t * 16, 16), 16), :]

    def reduce_mid(recv, tot, n, scale):
        wait(recv.at[0:15], p_r.at[2 * n])
        rows = pl.ds(pl.multiple_of(t * 16, 16), 16)
        tot[rows, :] = (scale * jnp.sum(recv[...], axis=0)).astype(BF16)

        def body(k, carry):
            send(tot.at[rows, :], tot.at[rows, :], p_s.at[2 * n + 1], p_r.at[2 * n + 1], (g, (t + k) % 16))
            return carry

        lax.fori_loop(1, 16, body, 0)

    def reduce_end(tot, half, n):
        wait(tot.at[0:240, :], p_r.at[2 * n + 1])
        for q in range(RUNS // 2):
            both = tot[q * RUN : (q + 1) * RUN, :].astype(F32)
            for side, r in ((0, q), (1, q + RUNS // 2)):
                x = jnp.where(upper == side, both, 0.0)
                x = x + pltpu.roll(x, RUN, 1)
                half[r * RUN : (r + 1) * RUN, :] = jnp.where(upper == sides[r], x, 0.0).astype(BF16)

    def run_rows(r):
        return slice(r * RUN, (r + 1) * RUN)

    def ring_far():
        wait(xr.at[0], x_r.at[0])
        x = acc[0] + decode(xr.at[0], ROWS)
        encode(x[:HALF_ROWS], zs_half.at[0])
        encode(x[HALF_ROWS:], zs_half.at[1])
        send(zs_half.at[0], zr_half.at[0], z_s.at[0], z_r.at[0], z_up)
        send(zs_half.at[1], zr_half.at[1], z_s.at[1], z_r.at[1], z_down)

    def ring(k):
        wait(xr.at[k], x_r.at[k])
        side = 1 - k % 2
        x = acc[k] + decode(xr.at[k], ROWS)
        if k < 3:
            wait(zr_half.at[side], z_r.at[side])
            got = decode(zr_half.at[side], HALF_ROWS)
            if side == 0:
                acc[k, 0:HALF_ROWS, :] = x[:HALF_ROWS] + got
                acc[k, HALF_ROWS:ROWS, :] = x[HALF_ROWS:]
            else:
                acc[k, 0:HALF_ROWS, :] = x[:HALF_ROWS]
                acc[k, HALF_ROWS:ROWS, :] = x[HALF_ROWS:] + got
            x = acc[k]
        else:
            wait(zr.at[k - 3], z_r.at[k - 1])
            x = x + decode(zr.at[k - 3], ROWS)
        encode(x, zs.at[k - 1])
        send(zs.at[k - 1], zr.at[k - 1], z_s.at[k + 1], z_r.at[k + 1], z_up if side == 0 else z_down)

    def scattered(half, b):
        return jnp.concatenate(
            [jnp.where(pairs[r] == b, half[run_rows(r), :], jnp.zeros((RUN, LANES), BF16)) for r in range(RUNS)],
            axis=0,
        )

    def order_y(m):
        j = m // 2
        return (j == 0) * 2 + (j == 1) * 1 + (j == 2) * 3

    def grad_pair(m, dc):
        weights = [scattered(half_b, gi(order_y(2 * m), dx, dc)) for dx in range(2)]
        x = nn(tok_t[...], jnp.concatenate(weights, axis=1))
        return x[:, :LANES], x[:, LANES:]

    def grad_out(m, carry):
        for dx, x in enumerate(grad_pair(m, 1)):
            encode(x, gcs.at[2 * m + dx])
        pair = pl.ds(2 * m, 2)
        send(gcs.at[pair], gcr.at[pair], gc_s.at[m], gc_r.at[m], core_peer)
        return carry

    def grad_own(m, carry):
        for dx, x in enumerate(grad_pair(m, 0)):
            gacc[2 * m + dx] = x
        return carry

    def grad_core(m):
        pair = pl.ds(2 * m, 2)
        wait(gcr.at[pair], gc_r.at[m])

    def grad_sum(m):
        return gacc[m] + decode(gcr.at[m], WIDTH)

    def grad_far(dx):
        x = grad_sum(dx)
        for way, to in enumerate((y_up, y_down)):
            i = 2 * way + dx
            encode(x[way * HALF_WIDTH : (way + 1) * HALF_WIDTH], gfs.at[i])
            send(gfs.at[i], gfr.at[i], gf_s.at[i], gf_r.at[i], to)

    def grad_near(way, dx):
        i, m = 2 * way + dx, 2 + 2 * way + dx
        wait(gfr.at[i], gf_r.at[i])
        x = grad_sum(m)
        far = decode(gfr.at[i], HALF_WIDTH)
        parts = [x[:HALF_WIDTH], x[HALF_WIDTH:]]
        parts[way] = parts[way] + far
        encode(jnp.concatenate(parts, axis=0), gys.at[i])
        send(gys.at[i], gyr.at[i], gy_s.at[i], gy_r.at[i], y_down if way else y_up)

    def grad_total(dx):
        wait(gyr.at[dx], gy_r.at[dx])
        wait(gyr.at[2 + dx], gy_r.at[2 + dx])
        return grad_sum(6 + dx) + decode(gyr.at[dx], WIDTH) + decode(gyr.at[2 + dx], WIDTH)

    def tg_part(n, carry):
        rows = pl.ds(pl.multiple_of(n * 256, 256), 256)
        frozen = nt(cotf[...], kv[rows, :])
        for r in range(RUNS):
            x = frozen[run_rows(r)] + nt(half_b[run_rows(r), :], dfull[pairs[r], rows, :])
            tg[run_rows(r), rows] = x.astype(BF16)
        return carry

    def up_pair(m, dc):
        weights = [scattered(half_d, gi(order_y(2 * m), dx, dc)) for dx in range(2)]
        x = 0.5 * nn(cot_t[...], jnp.concatenate(weights, axis=1))
        return x[:, :LANES], x[:, LANES:]

    def up_out(m, carry):
        for dx, x in enumerate(up_pair(m, 1)):
            ucs[2 * m + dx] = x
        return carry

    def up_own(m, carry):
        for dx, x in enumerate(up_pair(m, 0)):
            uacc[2 * m + dx] = x
        return carry

    for index in (6, 2, 1, 7, 3):
        up.to_core(index)
    down_a.handle(6, True)
    down_b.handle(2, False)
    handle_c(7)
    handle_c(1)
    for index in (4, 5):
        up.to_core(index)
    loads[0].wait()
    for index in range(8, 16):
        up.got(index)
    pack(lambda r: nt(cot[run_rows(r), :], ufull[pairs[r]]), part_b)
    reduce_start(part_b, recv_b, 0)
    base_send(0, 1)
    down_a.handle(1, True)
    handle_c(6)
    handle_c(2)
    down_b.handle(1, False)
    handle_c(8)
    down_b.handle(6, False)
    down_a.handle(2, True)

    reduce_mid(recv_b, tot_b, 0, 0.5)
    base_send(2, 3, 4, 5)
    down_a.handle(7, True)
    down_b.handle(3, False)
    handle_c(5)
    handle_c(3)
    ring_far()

    reduce_end(tot_b, half_b, 0)
    grad_out(0, 0)
    grad_own(0, 0)
    grad_out(1, 0)
    grad_core(0)
    grad_far(1)
    grad_far(0)
    handle_c(15)
    handle_c(9)
    grad_own(1, 0)
    lax.fori_loop(2, 4, grad_out, 0)
    lax.fori_loop(2, 4, grad_own, 0)
    down_b.handle(7, False)
    down_a.handle(3, True)
    for half_gather, upward in ((down_a, True), (down_b, False)):
        half_gather.handle(4, upward)
        half_gather.handle(5, upward)
    loads[4].wait()
    for index in range(8, 16):
        down_a.got(index)
        down_b.got(index)
    pack(lambda r: nn(tok[run_rows(r), :], dfull[pairs[r]]), part_d)
    reduce_start(part_d, recv_d, 1)
    base_send(6, 7)
    grad_core(1)
    grad_core(2)
    grad_near(0, 1)
    grad_near(1, 1)
    handle_c(14)
    handle_c(10)
    grad_near(0, 0)
    grad_near(1, 0)
    ring(1)
    ring(2)

    reduce_mid(recv_d, tot_d, 1, 1.0)
    handle_c(13)
    handle_c(11)
    ring(3)
    ring(4)
    grad_core(3)
    encode(grad_total(1), gxs)
    send(gxs, gxr, gx_s, gx_r, x_peer_g)

    reduce_end(tot_d, half_d, 1)
    lax.fori_loop(0, 4, up_out, 0)
    send(ucs, ucr, uc_s, uc_r, core_peer)
    lax.fori_loop(0, 4, up_own, 0)
    ring(5)
    ring(6)
    wait(ucr, uc_r)
    uacc[...] = uacc[...] + ucr[...]
    for i, m in enumerate((0, 1, 2, 3, 4, 5, 7)):
        dy, dx = Y_ORDER[m]
        encode(uacc[m], uds.at[i])
        send(uds.at[i], udr.at[i], ud_s.at[i], ud_r.at[i], (gi(dy, dx, 0), t))

    handle_c(4)
    handle_c(12)
    loads[5].wait()
    lax.fori_loop(0, WIDTH // 256, tg_part, 0)
    tg_out = pltpu.make_async_copy(tg, tg_h, out_sem.at[0])
    tg_out.start()
    dg[...] = grad_total(0)

    wait(xr.at[7], x_r.at[7])
    wait(zr.at[4], z_r.at[6])
    wait(zr.at[5], z_r.at[7])
    acc[7] = acc[7] + decode(xr.at[7], ROWS) + decode(zr.at[4], ROWS) + decode(zr.at[5], ROWS)
    for r in range(RUNS):
        lifted = nn(half_d[run_rows(r), :], ufull[pairs[r]])
        kvo[run_rows(r), :] = (acc[7, run_rows(r), :] + 0.5 * lifted).astype(BF16)
    kvo_out = pltpu.make_async_copy(kvo, kvo_h, out_sem.at[1])
    kvo_out.start()

    wait(gxr, gx_r)
    dg[...] = dg[...] + decode(gxr, WIDTH)
    dg_out = pltpu.make_async_copy(dg, dg_h, out_sem.at[3])
    dg_out.start()

    total = uacc[6]
    for i in range(7):
        wait(udr.at[i], ud_r.at[i])
        total = total + decode(udr.at[i], LANES)
    ug[...] = total.T
    ug_out = pltpu.make_async_copy(ug, ug_h, out_sem.at[2])
    ug_out.start()

    up.drain()
    down_a.drain()
    down_b.drain()
    for i in range(sent_c[0]):
        wait(cot_h, c_s.at[i])
    for k in range(8):
        wait(xs.at[k], x_s.at[k])
    for m in range(4):
        wait(gcs.at[pl.ds(2 * m, 2)], gc_s.at[m])
        wait(gfs.at[m], gf_s.at[m])
        wait(gys.at[m], gy_s.at[m])
    wait(zs_half.at[0], z_s.at[0])
    wait(zs_half.at[1], z_s.at[1])
    for k in range(6):
        wait(zs.at[k], z_s.at[k + 2])
    for n, (part, tot) in enumerate(((part_b, tot_b), (part_d, tot_d))):
        wait(part.at[0:240, :], p_s.at[2 * n])
        wait(tot.at[0:240, :], p_s.at[2 * n + 1])
    wait(gxs, gx_s)
    wait(ucs, uc_s)
    for i in range(7):
        wait(uds.at[i], ud_s.at[i])
    for copy in (tg_out, kvo_out, ug_out, dg_out):
        copy.wait()


def hand_over(*refs):
    sources, targets, staged, sem = refs[0:4], refs[4:8], refs[8:12], refs[12]
    pieces = []
    for i in (1, 2, 0, 3):
        rows = staged[i].shape[0]
        step = min(rows, 256)
        pieces += [(i, pl.ds(at, step)) for at in range(0, rows, step)]
    loads = [
        pltpu.make_async_copy(sources[i].at[rows, :], staged[i].at[rows, :], sem.at[0, n])
        for n, (i, rows) in enumerate(pieces)
    ]
    stores = [
        pltpu.make_async_copy(staged[i].at[rows, :], targets[i].at[rows, :], sem.at[1, n])
        for n, (i, rows) in enumerate(pieces)
    ]
    for load in loads:
        load.start()
    for load, store in zip(loads, stores):
        load.wait()
        store.start()
    for store in stores:
        store.wait()


def on_device(tokens, kv_weight, down_factors, up_factors, cotangent, adapter_ids, owner_slot):
    anywhere = pl.BlockSpec(memory_space=pl.ANY)
    scalars = pl.BlockSpec(memory_space=pltpu.SMEM)
    v = pltpu.VMEM
    i16 = jnp.int16
    dma = pltpu.SemaphoreType.DMA
    shape = jax.ShapeDtypeStruct
    out_shape = (
        shape((ROWS, LANES), BF16),
        shape((ROWS, WIDTH), BF16),
        shape((WIDTH, LANES), F32),
        shape((LANES, LANES), F32),
    )
    results = pl.pallas_call(
        kernel,
        out_shape=out_shape,
        in_specs=[scalars] * 2 + [anywhere] * 5,
        out_specs=(anywhere,) * 4,
        scratch_shapes=[
            v((ROWS, WIDTH), BF16),
            v((WIDTH, COLS), BF16),
            v((ROWS, LANES), BF16),
            v((ROWS, COLS), BF16),
            v((16, WIDTH, LANES), BF16),
            v((16, LANES, LANES), BF16),
            v((WIDTH, ROWS), BF16),
            v((LANES, ROWS), BF16),
            v((8, ROWS, LANES), F32),
            v((8, ROWS + EXTRA, LANES), i16),
            v((8, ROWS + EXTRA, LANES), i16),
            v((2, HALF_ROWS + EXTRA, LANES), i16),
            v((2, HALF_ROWS + EXTRA, LANES), i16),
            v((6, ROWS + EXTRA, LANES), i16),
            v((6, ROWS + EXTRA, LANES), i16),
            v((256, LANES), F32),
            v((16, 16, LANES), F32),
            v((256, LANES), BF16),
            v((256, LANES), F32),
            v((16, 16, LANES), F32),
            v((256, LANES), BF16),
            v((ROWS, LANES), BF16),
            v((ROWS, LANES), BF16),
            v((8, WIDTH, LANES), F32),
            v((8, WIDTH + EXTRA, LANES), i16),
            v((8, WIDTH + EXTRA, LANES), i16),
            v((4, HALF_WIDTH + EXTRA, LANES), i16),
            v((4, HALF_WIDTH + EXTRA, LANES), i16),
            v((4, WIDTH + EXTRA, LANES), i16),
            v((4, WIDTH + EXTRA, LANES), i16),
            v((WIDTH + EXTRA, LANES), i16),
            v((WIDTH + EXTRA, LANES), i16),
            v((8, LANES, LANES), F32),
            v((8, LANES, LANES), F32),
            v((8, LANES, LANES), F32),
            v((7, LANES + EXTRA, LANES), i16),
            v((7, LANES + EXTRA, LANES), i16),
            v((ROWS, LANES), BF16),
            v((ROWS, WIDTH), BF16),
            v((WIDTH, LANES), F32),
            v((LANES, LANES), F32),
            dma((6,)),
            dma((4,)),
            dma((15,)),
            dma((16,)),
            dma((15,)),
            dma((16,)),
            dma((15,)),
            dma((16,)),
            dma((15,)),
            dma((16,)),
            dma((8,)),
            dma((8,)),
            dma((8,)),
            dma((8,)),
            dma((4,)),
            dma((4,)),
            dma((4,)),
            dma((4,)),
            dma((4,)),
            dma((4,)),
            dma((4,)),
            dma((4,)),
            dma,
            dma,
            dma,
            dma,
            dma((7,)),
            dma((7,)),
        ],
        compiler_params=pltpu.CompilerParams(
            collective_id=0, has_side_effects=True, vmem_limit_bytes=56 * 1024 * 1024
        ),
    )(adapter_ids, owner_slot, tokens, kv_weight, down_factors, up_factors, cotangent)
    return pl.pallas_call(
        hand_over,
        out_shape=out_shape,
        in_specs=[anywhere] * 4,
        out_specs=(anywhere,) * 4,
        scratch_shapes=[v(o.shape, o.dtype) for o in out_shape] + [dma((2, 9))],
        compiler_params=pltpu.CompilerParams(vmem_limit_bytes=56 * 1024 * 1024),
    )(*results)


def solution(mesh):
    in_specs = (
        P("grp", "tp"),
        P("tp", None),
        P("tp", "grp"),
        P("grp", "tp"),
        P("grp", "tp"),
        P("grp"),
        P(),
    )
    out_specs = (P("grp", "tp"), P("grp", "tp"), P("tp", "grp"), P("grp", "tp"))
    return jax.shard_map(
        on_device, mesh=mesh, in_specs=in_specs, out_specs=out_specs, check_vma=False
    )
```
